256 devices in a mesh: north: 16 (over y, x), east: 8 (over z), group: 2 (over core).
Axes of the slice: x: 4, y: 4, z: 8, core: 2. Of those that a mesh axis runs over, the one named last changes fastest.
Arguments:
- alpha_fields: float32 [16, 8, 1024, 1024], P('group', None, 'north', 'east'), may hold values from -6 to 6
- perturbations: bfloat16 [16, 8, 1024, 1024], P('group', None, 'north', 'east'), may hold values from -6 to 6
- north_filter: float32 [5, 8, 1024], P(None, None, 'north'), may hold values from 0 to 1, as said below
- east_filter: float32 [5, 8, 1024], replicated, may hold values from 0 to 1, as said below
- depth_taps: float32 [5], replicated, may hold values from 0.3 to 1
Outputs:
- increment: float32 [8, 1024, 1024], P(None, 'north', 'east')
The draws below stay inside these ranges and needn't reach their ends.
Inputs may be any that keep to these rules, and one draw needn't show every extreme that they name: `north_filter`: entry 0 of the first dimension is a cell's gain, entries 1 to 4 its weights on the four preceding cells; the four weights of a cell are positive and sum to less than 1. `east_filter`: entry 0 of the first dimension is a cell's gain, entries 1 to 4 its weights on the four preceding cells; the four weights of a cell are positive and sum to less than 1.
All inputs are finite; a program needn't handle non-finite values.
Results may differ from the reference program's by a relative error of at most 0.0003.
Values may be sent and summed in bfloat16 or wider, within the bound.
No kernel may reach another device: no remote copies, remote signals or barrier semaphores. Data moves between devices by JAX's collectives and lax.ppermute only.
A program may use at most 128 MiB of HBM per device.

```python
import math
import jax
import jax.numpy as jnp
from jax import lax

MEMBERS = 16
LEV = 8
TAPS = 5
YN = 64
XE = 128
NY = 1024
NX = 1024


def line_filter(key, filter_lines, block, vertical_levels, fast_share):
    partition_keys = jax.random.split(key, 8)
    fast = jax.random.uniform(partition_keys[0], (vertical_levels, 1), jnp.float32) < fast_share
    fast_rate = min(2.5 / block, 0.05) * jax.random.uniform(partition_keys[1], (vertical_levels, 1), jnp.float32, 0.8, 1.25)
    slow_base = math.log(10.0) / filter_lines * jax.random.uniform(partition_keys[2], (vertical_levels, 1), jnp.float32, 0.1, 0.3)
    block_factor = jnp.exp(jax.random.uniform(partition_keys[3], (vertical_levels, filter_lines // block), jnp.float32, math.log(0.5), math.log(2.0)))
    slow_rate = slow_base * jnp.repeat(block_factor, block, axis=1)
    rate = jnp.where(fast, fast_rate, slow_rate)
    raw_weights = jax.random.uniform(partition_keys[4], (4, vertical_levels, filter_lines), jnp.float32, 0.5, 1.5)
    weights = raw_weights / jnp.sum(raw_weights, axis=0)
    lag_mean = jnp.sum(jnp.arange(1, 5, dtype=jnp.float32)[:, None, None] * weights, axis=0)
    retained_weight = 1.0 - rate * lag_mean
    spread_row_block = jax.random.randint(partition_keys[5], (vertical_levels, 2), 0, filter_lines)
    row_indices = jnp.arange(filter_lines, dtype=jnp.int32)[None, :]
    removed_entries = (row_indices == spread_row_block[:, 0:1]) | (row_indices == spread_row_block[:, 1:2])
    spread_retained = jax.random.uniform(partition_keys[6], (vertical_levels, filter_lines), jnp.float32, 0.65, 0.8)
    retained_weight = jnp.where(removed_entries, retained_weight * spread_retained, retained_weight)
    gains = math.sqrt(2.0) * lag_mean * rate ** 0.75 * jax.random.uniform(partition_keys[7], (vertical_levels, filter_lines), jnp.float32, 0.8, 1.25)
    return jnp.concatenate([gains[None], retained_weight[None] * weights], axis=0).astype(jnp.float32)


def draw_north_filter(key, part):
    fast_share = 0.5
    return line_filter(jax.random.fold_in(key, 11), NY, YN, LEV, fast_share)


def draw_east_filter(key, part):
    fast_share = 0.5
    return line_filter(jax.random.fold_in(key, 23), NX, XE, LEV, fast_share)


def draw_alpha_fields(key, part):
    first_key = jax.random.fold_in(jax.random.fold_in(key, 37), 0)
    shape = (MEMBERS, LEV, NY, NX)
    return jnp.clip(jax.random.normal(first_key, shape, jnp.float32), -6.0, 6.0)


def levels(key, shape, pieces, low, largest):
    def one(position, shards_of):
        draws = jax.random.uniform(jax.random.fold_in(jax.random.fold_in(key, 6), position), (shards_of,), jnp.float32, low / len(pieces), largest / len(pieces))
        return jnp.repeat(jnp.exp(draws), shape[position] // shards_of).reshape((-1,) + (1,) * (len(shape) - position - 1))

    level = one(*pieces[0])
    for cut in pieces[1:]:
        level = level * one(*cut)
    return level


def gaussian(rng, shape, spread, limit, pieces=(), kind=jnp.bfloat16):
    drawn = spread * jax.random.normal(rng, shape, jnp.float32)
    if pieces:
        drawn = drawn * levels(rng, shape, pieces, -0.22, 0.18)
    return jnp.clip(drawn, -limit, limit).astype(kind)


def setup_inputs(seed: int = 0) -> dict:
    key_list = jax.random.split(jax.random.key(seed), 6)
    return {
        "alpha_fields": draw_alpha_fields(jax.random.fold_in(key_list[5], 71), 0),
        "perturbations": gaussian(key_list[1], (MEMBERS, LEV, NY, NX), 1.0, 6.0, ((0, 2), (2, 16), (3, 8))),
        "north_filter": draw_north_filter(jax.random.fold_in(key_list[5], 71), 0),
        "east_filter": draw_east_filter(jax.random.fold_in(key_list[5], 71), 0),
        "depth_taps": jnp.clip(jax.random.uniform(key_list[4], (TAPS,), jnp.float32, 0.3, 1.0), 0.3, 1.0),
    }


highest = lax.Precision.HIGHEST

def forward_pass(data, table):
    gain_rows = jnp.transpose(table[0])
    weight_rows = jnp.transpose(table[1:5], (2, 0, 1))

    def advance(state, inputs):
        line_row, gain_row, weight_row = inputs
        value = gain_row[:, None] * line_row + lax.optimization_barrier(jnp.sum(weight_row[:, None, :, None] * state, axis=0))
        return (jnp.concatenate([value[None], state[:3]], axis=0), value)
    start = jnp.zeros((4,) + data.shape[1:], jnp.float32)
    _, result = lax.scan(advance, start, (data, gain_rows, weight_rows))
    return result

def adjoint_pass(data, table):
    extent = data.shape[0]
    padded = jnp.pad(table[1:5], ((0, 0), (0, 0), (0, 4)))
    shifted = jnp.stack([padded[offset, :, offset + 1:offset + 1 + extent] for offset in range(4)], axis=0)
    weight_rows = jnp.transpose(shifted, (2, 0, 1))
    gain_rows = jnp.transpose(table[0])

    def retreat(state, inputs):
        line_row, gain_row, weight_row = inputs
        value = line_row + lax.optimization_barrier(jnp.sum(weight_row[:, None, :, None] * state, axis=0))
        return (jnp.concatenate([value[None], state[:3]], axis=0), gain_row[:, None] * value)
    start = jnp.zeros((4,) + data.shape[1:], jnp.float32)
    _, result = lax.scan(retreat, start, (data, gain_rows, weight_rows), reverse=True)
    return result

def smooth_line(data, table):
    return adjoint_pass(forward_pass(data, table), table)

def depth_matrix(taps, vertical_levels):
    middle = (taps.shape[0] - 1) // 2
    row_indices = lax.broadcasted_iota(jnp.int32, (vertical_levels, vertical_levels), 0)
    col_ids = lax.broadcasted_iota(jnp.int32, (vertical_levels, vertical_levels), 1)
    mixing = jnp.zeros((vertical_levels, vertical_levels), jnp.float32)
    for offset in range(taps.shape[0]):
        mixing = mixing + jnp.where(col_ids - row_indices == offset - middle, taps[offset], 0.0)
    return mixing

def reference(alpha_fields, perturbations, north_filter, east_filter, depth_taps):
    northern = jnp.moveaxis(smooth_line(jnp.moveaxis(alpha_fields, 2, 0), north_filter), 0, 2)
    eastern = jnp.moveaxis(smooth_line(jnp.moveaxis(northern, 3, 0), east_filter), 0, 3)
    localized = jnp.einsum('kl,mlyx->mkyx', depth_matrix(depth_taps, LEV), eastern, precision=highest)
    scale = 1.0 / math.sqrt(MEMBERS - 1)
    return scale * lax.optimization_barrier(jnp.sum(perturbations.astype(jnp.float32) * localized, axis=0))
```

```python
import math

import jax
import jax.numpy as jnp
from jax import lax
from jax.experimental import pallas as pl
from jax.experimental.pallas import tpu as pltpu
from jax.sharding import PartitionSpec as P

F32 = jnp.float32
BF16 = jnp.bfloat16
VMEM = pl.BlockSpec(memory_space=pltpu.VMEM)
SMEM = pl.BlockSpec(memory_space=pltpu.SMEM)
HBM = pl.BlockSpec(memory_space=pltpu.HBM)
MIB = 1 << 20


def split(x):
    high = x.astype(BF16)
    return high, (x - high.astype(F32)).astype(BF16)


def split_rounded(x):
    high = x.astype(BF16).astype(F32)
    return high, x - high


def dot(a, b):
    return jnp.dot(a, b, preferred_element_type=F32)


def dot_nt(a, b):
    return lax.dot_general(a, b, (((1,), (1,)), ((), ())), preferred_element_type=F32)


def wide(column, lanes=128):
    return jnp.broadcast_to(column, (column.shape[0], lanes))


def lanes_of(rows=8, lanes=128):
    return lax.broadcasted_iota(jnp.int32, (rows, lanes), 1)


def rows_of(rows=8, lanes=128):
    return lax.broadcasted_iota(jnp.int32, (rows, lanes), 0)


def copies(source, target, sems, count):
    return [pltpu.make_async_copy(source.at[i], target.at[i], sems.at[i]) for i in range(count)]


def unit(mask):
    return jnp.where(mask, 1.0, 0.0).astype(F32)


def north_functionals(levels, members, rows):
    def kernel(
        nf_hbm, alpha_hbm, p_hbm, s_hbm, nf_ref, alpha_ref, f_ref, s_ref, p_ref, nf_sem, s_sem, sems, p_sems
    ):
        table_fetch = pltpu.make_async_copy(nf_hbm, nf_ref, nf_sem)
        table_fetch.start()
        fetches = copies(alpha_hbm, alpha_ref, sems, members)
        stores = copies(p_ref, p_hbm, p_sems, 2 * levels)
        slab_store = pltpu.make_async_copy(s_ref, s_hbm, s_sem)
        table_fetch.wait()
        for fetch in fetches:
            fetch.start()
        lane = lanes_of()
        table = [nf_ref[j] for j in range(5)]
        gain = jnp.concatenate([jnp.zeros((levels, 64), F32), table[0]], axis=1)
        state = [unit(lane == k) for k in range(4)]
        for i in range(rows):
            value = jnp.where(lane == 64 + i, gain, 0.0)
            for j in (4, 3, 2, 1):
                value = value + wide(table[j][:, i : i + 1]) * state[j - 1]
            f_ref[i] = value + unit(lane == 4 + rows - 1 - i) if i >= rows - 4 else value
            state = [value] + state[:3]
        state = [jnp.zeros((levels, 128), F32)] * 4
        for i in reversed(range(rows)):
            value = f_ref[i]
            for j in (4, 3, 2, 1):
                if i + j < rows:
                    value = value + wide(table[j][:, i + j : i + j + 1]) * state[j - 1]
            s_ref[i] = value * wide(table[0][:, i : i + 1])
            state = [value] + state[:3]
        slab_store.start()
        for fetch in fetches:
            fetch.wait()
        for l in range(levels):
            flat = f_ref[:, l, :]
            maps = jnp.dot(
                flat.T[0:8], flat, precision=lax.Precision.HIGHEST, preferred_element_type=F32
            )
            edge = s_ref[:, l, :].T[0:8]
            high, low = split_rounded(jnp.concatenate([edge, edge], axis=1))
            left = jnp.concatenate([high, low], axis=0).astype(BF16)
            for half in range(2):
                right = []
                for m in range(4):
                    a_high, a_low = split(alpha_ref[half * 4 + m, l])
                    right.append(jnp.concatenate([a_high, a_low], axis=0))
                out = dot(left, jnp.concatenate(right, axis=1))
                out = out[0:8] + out[8:16]
                for m in range(4):
                    p_ref[2 * l + half, 8 * m : 8 * m + 8, :] = out[:, 128 * m : 128 * m + 128]
                p_ref[2 * l + half, 32:40, :] = maps
                stores[2 * l + half].start()
        for store in stores + [slab_store]:
            store.wait()

    def call(north_filter, alpha):
        return pl.pallas_call(
            kernel,
            in_specs=[HBM, HBM],
            out_specs=[HBM, HBM],
            out_shape=[
                jax.ShapeDtypeStruct((2 * levels, 40, 128), F32),
                jax.ShapeDtypeStruct((rows, levels, 128), F32),
            ],
            scratch_shapes=[
                pltpu.VMEM(north_filter.shape, F32),
                pltpu.VMEM(alpha.shape, F32),
                pltpu.VMEM((rows, levels, 128), F32),
                pltpu.VMEM((rows, levels, 128), F32),
                pltpu.VMEM((2 * levels, 40, 128), F32),
                pltpu.SemaphoreType.DMA,
                pltpu.SemaphoreType.DMA,
                pltpu.SemaphoreType.DMA((members,)),
                pltpu.SemaphoreType.DMA((2 * levels,)),
            ],
            compiler_params=pltpu.CompilerParams(vmem_limit_bytes=63 * MIB),
            name="north_functionals",
        )(north_filter, alpha)

    return call


def chain_slabs(received):
    slabs = received.shape[0]

    def kernel(r_ref, z_ref, v_ref):
        state = [jnp.zeros((4, 128), F32)] * 4
        for n in range(slabs):
            maps = r_ref[n, 32:40, :]
            column = [wide(maps[:, j : j + 1]) for j in range(4)]
            for m in range(4):
                z_ref[n, 8 * m : 8 * m + 4, :] = state[m]
                value = r_ref[n, 8 * m : 8 * m + 8, :]
                for j in range(4):
                    value = value + column[j] * jnp.broadcast_to(state[m][j : j + 1], (8, 128))
                v_ref[n, 4 * m : 4 * m + 4, :] = value[0:4]
                state[m] = value[4:8]
        pending = [jnp.zeros((4, 128), F32)] * 4
        for n in reversed(range(slabs)):
            maps = r_ref[n, 32:36, :]
            column = [wide(maps[:, 4 + j : 5 + j]) for j in range(4)]
            for m in range(4):
                z_ref[n, 8 * m + 4 : 8 * m + 8, :] = pending[m]
                value = v_ref[n, 4 * m : 4 * m + 4, :]
                for j in range(4):
                    value = value + column[j] * jnp.broadcast_to(pending[m][j : j + 1], (4, 128))
                pending[m] = value

    return pl.pallas_call(
        kernel,
        in_specs=[VMEM],
        out_specs=VMEM,
        out_shape=jax.ShapeDtypeStruct((slabs, 32, 128), F32),
        scratch_shapes=[pltpu.VMEM((slabs, 16, 128), F32)],
        compiler_params=pltpu.CompilerParams(vmem_limit_bytes=8 * MIB),
        name="chain_slabs",
    )(received)


def north_slab(left, alpha_ref, l, members):
    for first in range(0, members, 4):
        right = []
        for m in range(first, first + 4):
            high, low = split(alpha_ref[m, l])
            right.append(jnp.concatenate([high, low, high, low], axis=0))
        yield first, dot(left, jnp.concatenate(right, axis=1))


def slab_left(full):
    twice = jnp.where(lanes_of(full.shape[0]) < 64, pltpu.roll(full, 64, 1), full)
    high, low = split(twice)
    return jnp.concatenate([high, low], axis=1)


def edge_right(z_ref, l, members):
    right = []
    for m in range(members):
        high, low = split_rounded(z_ref[l, 8 * m : 8 * m + 8, :])
        right.append(jnp.concatenate([high, low, high, low], axis=0).astype(BF16))
    return jnp.concatenate(right, axis=1)


def crossing_rows(v_ref, l, fields):
    parts = jnp.concatenate([jnp.concatenate(split(field), axis=1) for field in fields], axis=0)
    out = dot_nt(jnp.concatenate([v_ref[l], v_ref[l]], axis=1), parts)
    return out[0:32] + out[32:64]


def own_crossing(alpha, slab, sends):
    members, levels, rows, width = alpha.shape

    def kernel(alpha_hbm, s_ref, v_ref, c_ref, u_ref, b_ref, alpha_ref, sems):
        fetches = copies(alpha_hbm, alpha_ref, sems, members)
        for fetch in fetches:
            fetch.start()
        for fetch in fetches:
            fetch.wait()
        lane = lanes_of()
        for l in range(levels):
            full = s_ref[:, l, :]
            fields = []
            for _, out in north_slab(slab_left(full), alpha_ref, l, members):
                fields += [out[:, width * m : width * m + width] for m in range(4)]
            out = crossing_rows(v_ref, l, fields)
            for e in range(8):
                c_ref[e, 4 * l : 4 * l + 4, :] = out[4 * e : 4 * e + 4]
            high, low = split_rounded(full[:, 0:8])
            u_ref[l] = jnp.concatenate([high, high, low, low], axis=1).astype(BF16)
            edge = full.T[0:8]
            edge = jnp.concatenate([edge, edge], axis=1)
            edge = jnp.concatenate([jnp.where(lane < 64, edge, 0.0), jnp.where(lane < 64, 0.0, edge)], axis=0)
            b_ref[l] = jnp.concatenate(split(edge), axis=0)

    return pl.pallas_call(
        kernel,
        in_specs=[HBM, VMEM, VMEM],
        out_specs=[VMEM] * 3,
        scratch_shapes=[pltpu.VMEM(alpha.shape, F32), pltpu.SemaphoreType.DMA((members,))],
        out_shape=[
            jax.ShapeDtypeStruct((8, 4 * levels, members * rows), F32),
            jax.ShapeDtypeStruct((levels, rows, 32), BF16),
            jax.ShapeDtypeStruct((levels, 32, 128), BF16),
        ],
        compiler_params=pltpu.CompilerParams(vmem_limit_bytes=16 * MIB),
        cost_estimate=pl.CostEstimate(flops=2_000_000_000, bytes_accessed=4 * MIB, transcendentals=0),
        name="own_crossing",
    )(alpha, slab, sends)


def east_matrices(place, taps, east_filter, scale):
    levels = east_filter.shape[1]
    length = 128
    slabs = east_filter.shape[2] // length

    def kernel(e_ref, taps_ref, ef_ref, e_out, v_out, w_out, wt_ref, rt_ref, f_ref, s_ref):
        me = e_ref[0]
        lane = lanes_of()
        row = rows_of()
        for j in range(1, 5):
            stacked = jnp.concatenate(
                [ef_ref[j, :, length * s : length * (s + 1)] for s in range(slabs)] * 2, axis=0
            )
            wt_ref[j - 1] = stacked.T
        state = [unit(row == k) for k in range(4)]
        gram = [jnp.zeros((8, 128), F32)] * 4
        for i in range(length):
            value = jnp.zeros((8, 128), F32)
            for j in (3, 2, 1, 0):
                value = value + jnp.broadcast_to(wt_ref[j, i : i + 1, :], (8, 128)) * state[j]
            gram = [gram[k] + value * jnp.broadcast_to(value[k : k + 1], (8, 128)) for k in range(4)]
            state = [value] + state[:3]
        step = state
        reflect = [jnp.zeros((8, 128), F32)] * 4
        for _ in range(slabs - 1):
            inner = [
                sum(jnp.broadcast_to(reflect[i][j : j + 1], (8, 128)) * step[j] for j in range(4))
                for i in range(4)
            ]
            outer = [
                gram[a]
                + sum(jnp.broadcast_to(step[i][a : a + 1], (8, 128)) * inner[i] for i in range(4))
                for a in range(4)
            ]
            reflect = [jnp.where(lane < 56, pltpu.roll(outer[a], 120, 1), 0.0) for a in range(4)]
        rt_ref[...] = jnp.concatenate(reflect * 4, axis=0).T
        back = rt_ref[pl.ds(pl.multiple_of(me * 8, 8), 8), :]
        own = [ef_ref[j, :, pl.ds(pl.multiple_of(me * length, length), length)] for j in range(5)]
        core = [jnp.zeros((levels, 128), F32)] * 4
        side = [unit(lane == k) for k in range(4)]
        for i in range(length):
            weight = [wide(own[j][:, i : i + 1]) for j in range(1, 5)]
            c_value = jnp.where(lane == i, own[0], 0.0)
            s_value = jnp.zeros((levels, 128), F32)
            for j in (3, 2, 1, 0):
                c_value = c_value + weight[j] * core[j]
                s_value = s_value + weight[j] * side[j]
            f_ref[i, :, 0:128] = c_value
            f_ref[i, :, 128:256] = s_value
            core = [c_value] + core[:3]
            side = [s_value] + side[:3]
        for k in range(4):
            c_value, s_value = core[k], side[k]
            for j in range(4):
                weight = wide(back[:, 8 * k + j : 8 * k + j + 1])
                c_value = c_value + weight * core[j]
                s_value = s_value + weight * side[j]
            f_ref[length - 1 - k, :, 0:128] = c_value
            f_ref[length - 1 - k, :, 128:256] = s_value + unit(lane == 4 + k)
        core = [jnp.zeros((levels, 128), F32)] * 4
        side = [jnp.zeros((levels, 128), F32)] * 4
        for i in reversed(range(length)):
            c_value = f_ref[i, :, 0:128]
            s_value = f_ref[i, :, 128:256]
            for j in (4, 3, 2, 1):
                if i + j < length:
                    weight = wide(own[j][:, i + j : i + j + 1])
                    c_value = c_value + weight * core[j - 1]
                    s_value = s_value + weight * side[j - 1]
            gain = wide(own[0][:, i : i + 1])
            s_ref[i, :, 0:128] = c_value * gain
            s_ref[i, :, 128:256] = s_value * gain
            core = [c_value] + core[:3]
            side = [s_value] + side[:3]
        across = [
            jnp.concatenate([step[i][j : j + 1] for i in range(4)], axis=0) for j in range(4)
        ]
        entering, pending = [], []
        for l in range(levels):
            e_high, e_low = split(s_ref[:, l, 0:128])
            e_out[l] = jnp.concatenate([e_high, e_low], axis=0)
            edge = s_ref[:, l, 128:256].T[0:8]
            start, end = edge[0:4], edge[4:8]
            entering.append(start)
            pending.append(end)
            upward = [end]
            for e in range(1, slabs):
                at = 8 * (e - 1) + l
                moved = sum(
                    wide(across[j][:, at : at + 1]) * jnp.broadcast_to(upward[-1][j : j + 1], (4, 128))
                    for j in range(4)
                )
                upward.append(jnp.where(e - 1 > me, moved, end))
            downward = [start]
            for e in reversed(range(slabs - 1)):
                at = 8 * (e + 1) + l
                moved = sum(
                    wide(step[j][0:4, at : at + 1])
                    * jnp.broadcast_to(downward[-1][j : j + 1], (4, 128))
                    for j in range(4)
                )
                downward.append(jnp.where(e + 1 < me, moved, start))
            downward.reverse()
            sends = jnp.concatenate(
                [jnp.where(e > me, upward[e], downward[e]) for e in range(slabs)], axis=0
            )
            high, low = split_rounded(sends)
            v_out[l] = jnp.concatenate([high, low], axis=0).astype(BF16)
        columns = jnp.concatenate(entering + pending, axis=0)
        level = lax.rem(rows_of(64), 32) // 4
        for k in range(levels):
            mix = jnp.zeros((64, 128), F32)
            for offset in range(5):
                mix = mix + jnp.where(level - k == offset - 2, taps_ref[offset] * scale, 0.0)
            high, low = split(columns * mix)
            w_out[:, 128 * k : 128 * k + 128] = jnp.concatenate([high, low], axis=0)

    return pl.pallas_call(
        kernel,
        in_specs=[SMEM, SMEM, VMEM],
        out_specs=[VMEM, VMEM, VMEM],
        out_shape=[
            jax.ShapeDtypeStruct((levels, 2 * length, length), BF16),
            jax.ShapeDtypeStruct((levels, 64, length), BF16),
            jax.ShapeDtypeStruct((128, levels * length), BF16),
        ],
        scratch_shapes=[
            pltpu.VMEM((4, 128, 128), F32),
            pltpu.VMEM((128, 128), F32),
            pltpu.VMEM((length, levels, 256), F32),
            pltpu.VMEM((length, levels, 256), F32),
        ],
        compiler_params=pltpu.CompilerParams(vmem_limit_bytes=16 * MIB),
        cost_estimate=pl.CostEstimate(flops=2_000_000_000, bytes_accessed=4 * MIB, transcendentals=0),
        name="east_matrices",
    )(place, taps, east_filter)


def north_finish(own, edges, entered, sends):
    levels = edges.shape[0]
    pairs = entered.shape[1] // 16

    def kernel(c0_ref, b_ref, z_ref, v_ref, c_hbm, c_ref, sems):
        stores = [
            pltpu.make_async_copy(
                c_ref.at[:, pl.ds(8 * j, 8)], c_hbm.at[:, pl.ds(8 * j, 8)], sems.at[j]
            )
            for j in range(levels // 2)
        ]
        empty = jnp.zeros((16, 128), BF16)
        for l in range(levels):
            values = [
                jnp.concatenate(split(z_ref[l, 16 * p : 16 * p + 16, :]), axis=1) for p in range(pairs)
            ]
            out = dot_nt(
                jnp.concatenate([v_ref[l], v_ref[l]], axis=1), jnp.concatenate(values * 2, axis=0)
            )
            high, low = split_rounded(out[0:32] + out[32:64])
            left = jnp.where(lanes_of(32) < 64, high, low).astype(BF16)
            left = jnp.concatenate([left, left], axis=1)
            blocks = [
                jnp.concatenate(
                    [
                        jnp.concatenate([piece if p == q else empty for q in range(pairs)], axis=1)
                        for p in range(pairs)
                    ],
                    axis=0,
                )
                for piece in (b_ref[l, 0:16], b_ref[l, 16:32])
            ]
            out = dot(left, jnp.concatenate([blocks[0], blocks[0], blocks[1], blocks[1]], axis=0))
            for e in range(8):
                at = slice(4 * l, 4 * l + 4)
                c_ref[e, at, :] = c0_ref[e, at, :] + out[4 * e : 4 * e + 4]
            if l % 2:
                stores[l // 2].start()
        for store in stores:
            store.wait()

    return pl.pallas_call(
        kernel,
        in_specs=[VMEM] * 4,
        out_specs=HBM,
        out_shape=jax.ShapeDtypeStruct(own.shape, F32),
        scratch_shapes=[pltpu.VMEM(own.shape, F32), pltpu.SemaphoreType.DMA((levels // 2,))],
        compiler_params=pltpu.CompilerParams(vmem_limit_bytes=16 * MIB),
        name="north_finish",
    )(own, edges, entered, sends)


def own_increment(taps, alpha, slab, columns, entered, east, perturbations, scale):
    members, levels, rows, width = alpha.shape

    def kernel(taps_ref, alpha_hbm, slab_ref, u_ref, z_ref, e_ref, pert_ref, out_ref, keep_ref, alpha_ref, s_ref, sems):
        fetches = copies(alpha_hbm, alpha_ref, sems, members)
        for fetch in fetches:
            fetch.start()
        for fetch in fetches:
            fetch.wait()
        for l in range(levels):
            added = dot(u_ref[l], edge_right(z_ref, l, members))
            for first, out in north_slab(slab_left(slab_ref[:, l, :]), alpha_ref, l, members):
                out = out + added[:, width * first : width * (first + 4)]
                field = jnp.concatenate([out[:, width * m : width * m + width] for m in range(4)], axis=0)
                high, low = split(field)
                e_high = e_ref[l, 0:width]
                s_ref[l, rows * first : rows * (first + 4)] = dot(
                    jnp.concatenate([high, low], axis=1), jnp.concatenate([e_high, e_high], axis=0)
                ) + dot(high, e_ref[l, width : 2 * width])
        tap = [taps_ref[o] * scale for o in range(5)]
        for k in range(levels):
            total = jnp.zeros((rows, width), F32)
            for m in range(members):
                mixed = sum(
                    tap[o] * s_ref[k + o - 2, rows * m : rows * m + rows, :]
                    for o in range(5)
                    if 0 <= k + o - 2 < levels
                )
                total = total + pert_ref[m, k].astype(F32) * mixed
            out_ref[k] = total
        keep_ref[...] = pert_ref[...]

    return pl.pallas_call(
        kernel,
        in_specs=[SMEM, HBM] + [VMEM] * 5,
        out_specs=[VMEM, VMEM],
        out_shape=[
            jax.ShapeDtypeStruct((levels, rows, width), F32),
            jax.ShapeDtypeStruct(perturbations.shape, BF16),
        ],
        scratch_shapes=[
            pltpu.VMEM(alpha.shape, F32),
            pltpu.VMEM((levels, members * rows, width), F32),
            pltpu.SemaphoreType.DMA((members,)),
        ],
        compiler_params=pltpu.CompilerParams(vmem_limit_bytes=24 * MIB),
        cost_estimate=pl.CostEstimate(flops=2_000_000_000, bytes_accessed=4 * MIB, transcendentals=0),
        name="own_increment",
    )(taps, alpha, slab, columns, entered, east, perturbations)


def finish(place, received, columns, perturbations, partial):
    members, levels, rows, width = perturbations.shape
    slabs = received.shape[0]

    def kernel(e_ref, r_ref, w_ref, pert_ref, part_ref, out_ref):
        me = e_ref[0]
        entering = jnp.zeros(r_ref.shape[1:], F32)
        pending = jnp.zeros(r_ref.shape[1:], F32)
        for s in range(slabs):
            block = r_ref[s]
            entering = entering + jnp.where(s < me, block, 0.0)
            pending = pending + jnp.where(s > me, block, 0.0)
        edge = jnp.concatenate([entering, pending] * 2, axis=0).T
        high, low = split_rounded(edge)
        left = jnp.where(lanes_of(members * rows) < 64, high, low).astype(BF16)
        left = jnp.concatenate([left, left], axis=1)
        for k in range(levels):
            out_ref[k] = part_ref[k]
        high, low = w_ref[0:64], w_ref[64:128]
        right = jnp.concatenate([high, high, low, low], axis=0)
        for m in range(members):
            added = dot(left[rows * m : rows * m + rows], right)
            for k in range(levels):
                out_ref[k] += pert_ref[m, k].astype(F32) * added[:, width * k : width * k + width]

    return pl.pallas_call(
        kernel,
        in_specs=[SMEM] + [VMEM] * 4,
        out_specs=VMEM,
        out_shape=jax.ShapeDtypeStruct((levels, rows, width), F32),
        compiler_params=pltpu.CompilerParams(vmem_limit_bytes=16 * MIB),
        name="finish",
    )(place, received, columns, perturbations, partial)


def local(alpha_fields, perturbations, north_filter, east_filter, depth_taps):
    members, levels, rows, width = alpha_fields.shape
    scale = 1.0 / math.sqrt(members * lax.axis_size("group") - 1)
    place = jnp.full((1,), lax.axis_index("east"), jnp.int32)
    functionals, slab = north_functionals(levels, members, rows)(north_filter, alpha_fields)
    gathered = lax.all_to_all(functionals, "north", 0, 0)
    east, sends, columns = east_matrices(place, depth_taps, east_filter, scale)
    gathered, sends = lax.optimization_barrier((gathered, sends))
    chained, slab = lax.optimization_barrier((chain_slabs(gathered), slab))
    entered = lax.all_to_all(chained, "north", 0, 0).reshape(levels, 8 * members, width)
    own, edge, blocks = own_crossing(alpha_fields, slab, sends)
    crossing = north_finish(own, blocks, entered, sends)
    crossing, entered = lax.optimization_barrier((crossing, entered))
    crossed = lax.all_to_all(crossing, "east", 0, 0)
    partial, kept = own_increment(depth_taps, alpha_fields, slab, edge, entered, east, perturbations, scale)
    increment = finish(place, crossed, columns, kept, partial)
    return increment + lax.ppermute(increment, "group", [(0, 1), (1, 0)])


def solution(mesh):
    placed = (
        P("group", None, "north", "east"),
        P("group", None, "north", "east"),
        P(None, None, "north"),
        P(),
        P(),
    )
    return jax.shard_map(
        local, mesh=mesh, in_specs=placed, out_specs=P(None, "north", "east"), check_vma=False
    )
```

```python
import math

import jax
import jax.numpy as jnp
from jax import lax
from jax.experimental import pallas as pl
from jax.experimental.pallas import tpu as pltpu
from jax.sharding import PartitionSpec as P

F32 = jnp.float32
BF16 = jnp.bfloat16
VMEM = pl.BlockSpec(memory_space=pltpu.VMEM)
SMEM = pl.BlockSpec(memory_space=pltpu.SMEM)
HBM = pl.BlockSpec(memory_space=pltpu.HBM)
MIB = 1 << 20


def split(x):
    high = x.astype(BF16)
    return high, (x - high.astype(F32)).astype(BF16)


def split_rounded(x):
    high = x.astype(BF16).astype(F32)
    return high, x - high


def dot(a, b):
    return jnp.dot(a, b, preferred_element_type=F32)


def dot_nt(a, b):
    return lax.dot_general(a, b, (((1,), (1,)), ((), ())), preferred_element_type=F32)


def wide(column, lanes=128):
    return jnp.broadcast_to(column, (column.shape[0], lanes))


def lanes_of(rows=8, lanes=128):
    return lax.broadcasted_iota(jnp.int32, (rows, lanes), 1)


def rows_of(rows=8, lanes=128):
    return lax.broadcasted_iota(jnp.int32, (rows, lanes), 0)


def copies(source, target, sems, count):
    return [pltpu.make_async_copy(source.at[i], target.at[i], sems.at[i]) for i in range(count)]


def unit(mask):
    return jnp.where(mask, 1.0, 0.0).astype(F32)


def north_functionals(levels, members, rows):
    def kernel(
        nf_hbm, alpha_hbm, p_hbm, s_hbm, nf_ref, alpha_ref, f_ref, s_ref, p_ref, nf_sem, s_sem, sems, p_sems
    ):
        table_fetch = pltpu.make_async_copy(nf_hbm, nf_ref, nf_sem)
        table_fetch.start()
        fetches = copies(alpha_hbm, alpha_ref, sems, members)
        stores = copies(p_ref, p_hbm, p_sems, 2 * levels)
        slab_store = pltpu.make_async_copy(s_ref, s_hbm, s_sem)
        for fetch in fetches:
            fetch.start()
        table_fetch.wait()
        lane = lanes_of()
        table = [nf_ref[j] for j in range(5)]
        gain = jnp.concatenate([jnp.zeros((levels, 64), F32), table[0]], axis=1)
        state = [unit(lane == k) for k in range(4)]
        for i in range(rows):
            value = jnp.where(lane == 64 + i, gain, 0.0)
            for j in (4, 3, 2, 1):
                value = value + wide(table[j][:, i : i + 1]) * state[j - 1]
            f_ref[i] = value + unit(lane == 4 + rows - 1 - i) if i >= rows - 4 else value
            state = [value] + state[:3]
        state = [jnp.zeros((levels, 128), F32)] * 4
        for i in reversed(range(rows)):
            value = f_ref[i]
            for j in (4, 3, 2, 1):
                if i + j < rows:
                    value = value + wide(table[j][:, i + j : i + j + 1]) * state[j - 1]
            s_ref[i] = value * wide(table[0][:, i : i + 1])
            state = [value] + state[:3]
        slab_store.start()
        for fetch in fetches:
            fetch.wait()
        for l in range(levels):
            flat = f_ref[:, l, :]
            maps = jnp.dot(
                flat.T[0:8], flat, precision=lax.Precision.HIGHEST, preferred_element_type=F32
            )
            edge = s_ref[:, l, :].T[0:8]
            high, low = split_rounded(jnp.concatenate([edge, edge], axis=1))
            left = jnp.concatenate([high, low], axis=0).astype(BF16)
            for half in range(2):
                right = []
                for m in range(4):
                    a_high, a_low = split(alpha_ref[half * 4 + m, l])
                    right.append(jnp.concatenate([a_high, a_low], axis=0))
                out = dot(left, jnp.concatenate(right, axis=1))
                out = out[0:8] + out[8:16]
                for m in range(4):
                    p_ref[2 * l + half, 8 * m : 8 * m + 8, :] = out[:, 128 * m : 128 * m + 128]
                p_ref[2 * l + half, 32:40, :] = maps
                stores[2 * l + half].start()
        for store in stores + [slab_store]:
            store.wait()

    def call(north_filter, alpha):
        return pl.pallas_call(
            kernel,
            in_specs=[HBM, HBM],
            out_specs=[HBM, HBM],
            out_shape=[
                jax.ShapeDtypeStruct((2 * levels, 40, 128), F32),
                jax.ShapeDtypeStruct((rows, levels, 128), F32),
            ],
            scratch_shapes=[
                pltpu.VMEM(north_filter.shape, F32),
                pltpu.VMEM(alpha.shape, F32),
                pltpu.VMEM((rows, levels, 128), F32),
                pltpu.VMEM((rows, levels, 128), F32),
                pltpu.VMEM((2 * levels, 40, 128), F32),
                pltpu.SemaphoreType.DMA,
                pltpu.SemaphoreType.DMA,
                pltpu.SemaphoreType.DMA((members,)),
                pltpu.SemaphoreType.DMA((2 * levels,)),
            ],
            compiler_params=pltpu.CompilerParams(vmem_limit_bytes=63 * MIB),
            name="north_functionals",
        )(north_filter, alpha)

    return call


def chain_slabs(received):
    slabs = received.shape[0]

    def kernel(r_ref, z_ref, v_ref):
        state = [jnp.zeros((4, 128), F32)] * 4
        for n in range(slabs):
            maps = r_ref[n, 32:40, :]
            column = [wide(maps[:, j : j + 1]) for j in range(4)]
            for m in range(4):
                z_ref[n, 8 * m : 8 * m + 4, :] = state[m]
                value = r_ref[n, 8 * m : 8 * m + 8, :]
                for j in range(4):
                    value = value + column[j] * jnp.broadcast_to(state[m][j : j + 1], (8, 128))
                v_ref[n, 4 * m : 4 * m + 4, :] = value[0:4]
                state[m] = value[4:8]
        pending = [jnp.zeros((4, 128), F32)] * 4
        for n in reversed(range(slabs)):
            maps = r_ref[n, 32:36, :]
            column = [wide(maps[:, 4 + j : 5 + j]) for j in range(4)]
            for m in range(4):
                z_ref[n, 8 * m + 4 : 8 * m + 8, :] = pending[m]
                value = v_ref[n, 4 * m : 4 * m + 4, :]
                for j in range(4):
                    value = value + column[j] * jnp.broadcast_to(pending[m][j : j + 1], (4, 128))
                pending[m] = value

    return pl.pallas_call(
        kernel,
        in_specs=[VMEM],
        out_specs=VMEM,
        out_shape=jax.ShapeDtypeStruct((slabs, 32, 128), F32),
        scratch_shapes=[pltpu.VMEM((slabs, 16, 128), F32)],
        compiler_params=pltpu.CompilerParams(vmem_limit_bytes=8 * MIB),
        name="chain_slabs",
    )(received)


def north_slab(left, alpha_ref, l, members):
    for first in range(0, members, 4):
        right = []
        for m in range(first, first + 4):
            high, low = split(alpha_ref[m, l])
            right.append(jnp.concatenate([high, low, high, low], axis=0))
        yield first, dot(left, jnp.concatenate(right, axis=1))


def slab_left(full):
    twice = jnp.where(lanes_of(full.shape[0]) < 64, pltpu.roll(full, 64, 1), full)
    high, low = split(twice)
    return jnp.concatenate([high, low], axis=1)


def edge_right(z_ref, l, members):
    right = []
    for m in range(members):
        high, low = split_rounded(z_ref[l, 8 * m : 8 * m + 8, :])
        right.append(jnp.concatenate([high, low, high, low], axis=0).astype(BF16))
    return jnp.concatenate(right, axis=1)


def crossing_rows(v_ref, l, fields):
    parts = jnp.concatenate([jnp.concatenate(split(field), axis=1) for field in fields], axis=0)
    out = dot_nt(jnp.concatenate([v_ref[l], v_ref[l]], axis=1), parts)
    return out[0:32] + out[32:64]


def own_crossing(alpha, slab, sends):
    members, levels, rows, width = alpha.shape

    def kernel(alpha_hbm, s_ref, v_ref, c_ref, u_ref, b_ref, alpha_ref, sems):
        fetches = copies(alpha_hbm, alpha_ref, sems, members)
        for fetch in fetches:
            fetch.start()
        for fetch in fetches:
            fetch.wait()
        lane = lanes_of()
        for l in range(levels):
            full = s_ref[:, l, :]
            fields = []
            for _, out in north_slab(slab_left(full), alpha_ref, l, members):
                fields += [out[:, width * m : width * m + width] for m in range(4)]
            out = crossing_rows(v_ref, l, fields)
            for e in range(8):
                c_ref[e, 4 * l : 4 * l + 4, :] = out[4 * e : 4 * e + 4]
            high, low = split_rounded(full[:, 0:8])
            u_ref[l] = jnp.concatenate([high, high, low, low], axis=1).astype(BF16)
            edge = full.T[0:8]
            edge = jnp.concatenate([edge, edge], axis=1)
            edge = jnp.concatenate([jnp.where(lane < 64, edge, 0.0), jnp.where(lane < 64, 0.0, edge)], axis=0)
            b_ref[l] = jnp.concatenate(split(edge), axis=0)

    return pl.pallas_call(
        kernel,
        in_specs=[HBM, VMEM, VMEM],
        out_specs=[VMEM] * 3,
        scratch_shapes=[pltpu.VMEM(alpha.shape, F32), pltpu.SemaphoreType.DMA((members,))],
        out_shape=[
            jax.ShapeDtypeStruct((8, 4 * levels, members * rows), F32),
            jax.ShapeDtypeStruct((levels, rows, 32), BF16),
            jax.ShapeDtypeStruct((levels, 32, 128), BF16),
        ],
        compiler_params=pltpu.CompilerParams(vmem_limit_bytes=16 * MIB),
        cost_estimate=pl.CostEstimate(flops=2_000_000_000, bytes_accessed=4 * MIB, transcendentals=0),
        name="own_crossing",
    )(alpha, slab, sends)


def east_matrices(place, taps, east_filter, scale):
    levels = east_filter.shape[1]
    length = 128
    slabs = east_filter.shape[2] // length

    def kernel(e_ref, taps_ref, ef_ref, e_out, v_out, w_out, wt_ref, rt_ref, f_ref, s_ref):
        me = e_ref[0]
        lane = lanes_of()
        row = rows_of()
        for j in range(1, 5):
            stacked = jnp.concatenate(
                [ef_ref[j, :, length * s : length * (s + 1)] for s in range(slabs)] * 2, axis=0
            )
            wt_ref[j - 1] = stacked.T
        state = [unit(row == k) for k in range(4)]
        gram = [jnp.zeros((8, 128), F32)] * 4
        for i in range(length):
            value = jnp.zeros((8, 128), F32)
            for j in (3, 2, 1, 0):
                value = value + jnp.broadcast_to(wt_ref[j, i : i + 1, :], (8, 128)) * state[j]
            gram = [gram[k] + value * jnp.broadcast_to(value[k : k + 1], (8, 128)) for k in range(4)]
            state = [value] + state[:3]
        step = state
        reflect = [jnp.zeros((8, 128), F32)] * 4
        for _ in range(slabs - 1):
            inner = [
                sum(jnp.broadcast_to(reflect[i][j : j + 1], (8, 128)) * step[j] for j in range(4))
                for i in range(4)
            ]
            outer = [
                gram[a]
                + sum(jnp.broadcast_to(step[i][a : a + 1], (8, 128)) * inner[i] for i in range(4))
                for a in range(4)
            ]
            reflect = [jnp.where(lane < 56, pltpu.roll(outer[a], 120, 1), 0.0) for a in range(4)]
        rt_ref[...] = jnp.concatenate(reflect * 4, axis=0).T
        back = rt_ref[pl.ds(pl.multiple_of(me * 8, 8), 8), :]
        own = [ef_ref[j, :, pl.ds(pl.multiple_of(me * length, length), length)] for j in range(5)]
        core = [jnp.zeros((levels, 128), F32)] * 4
        side = [unit(lane == k) for k in range(4)]
        for i in range(length):
            weight = [wide(own[j][:, i : i + 1]) for j in range(1, 5)]
            c_value = jnp.where(lane == i, own[0], 0.0)
            s_value = jnp.zeros((levels, 128), F32)
            for j in (3, 2, 1, 0):
                c_value = c_value + weight[j] * core[j]
                s_value = s_value + weight[j] * side[j]
            f_ref[i, :, 0:128] = c_value
            f_ref[i, :, 128:256] = s_value
            core = [c_value] + core[:3]
            side = [s_value] + side[:3]
        for k in range(4):
            c_value, s_value = core[k], side[k]
            for j in range(4):
                weight = wide(back[:, 8 * k + j : 8 * k + j + 1])
                c_value = c_value + weight * core[j]
                s_value = s_value + weight * side[j]
            f_ref[length - 1 - k, :, 0:128] = c_value
            f_ref[length - 1 - k, :, 128:256] = s_value + unit(lane == 4 + k)
        core = [jnp.zeros((levels, 128), F32)] * 4
        side = [jnp.zeros((levels, 128), F32)] * 4
        for i in reversed(range(length)):
            c_value = f_ref[i, :, 0:128]
            s_value = f_ref[i, :, 128:256]
            for j in (4, 3, 2, 1):
                if i + j < length:
                    weight = wide(own[j][:, i + j : i + j + 1])
                    c_value = c_value + weight * core[j - 1]
                    s_value = s_value + weight * side[j - 1]
            gain = wide(own[0][:, i : i + 1])
            s_ref[i, :, 0:128] = c_value * gain
            s_ref[i, :, 128:256] = s_value * gain
            core = [c_value] + core[:3]
            side = [s_value] + side[:3]
        across = [
            jnp.concatenate([step[i][j : j + 1] for i in range(4)], axis=0) for j in range(4)
        ]
        entering, pending = [], []
        for l in range(levels):
            e_high, e_low = split(s_ref[:, l, 0:128])
            e_out[l] = jnp.concatenate([e_high, e_low], axis=0)
            edge = s_ref[:, l, 128:256].T[0:8]
            start, end = edge[0:4], edge[4:8]
            entering.append(start)
            pending.append(end)
            upward = [end]
            for e in range(1, slabs):
                at = 8 * (e - 1) + l
                moved = sum(
                    wide(across[j][:, at : at + 1]) * jnp.broadcast_to(upward[-1][j : j + 1], (4, 128))
                    for j in range(4)
                )
                upward.append(jnp.where(e - 1 > me, moved, end))
            downward = [start]
            for e in reversed(range(slabs - 1)):
                at = 8 * (e + 1) + l
                moved = sum(
                    wide(step[j][0:4, at : at + 1])
                    * jnp.broadcast_to(downward[-1][j : j + 1], (4, 128))
                    for j in range(4)
                )
                downward.append(jnp.where(e + 1 < me, moved, start))
            downward.reverse()
            sends = jnp.concatenate(
                [jnp.where(e > me, upward[e], downward[e]) for e in range(slabs)], axis=0
            )
            high, low = split_rounded(sends)
            v_out[l] = jnp.concatenate([high, low], axis=0).astype(BF16)
        columns = jnp.concatenate(entering + pending, axis=0)
        level = lax.rem(rows_of(64), 32) // 4
        for k in range(levels):
            mix = jnp.zeros((64, 128), F32)
            for offset in range(5):
                mix = mix + jnp.where(level - k == offset - 2, taps_ref[offset] * scale, 0.0)
            high, low = split(columns * mix)
            w_out[:, 128 * k : 128 * k + 128] = jnp.concatenate([high, low], axis=0)

    return pl.pallas_call(
        kernel,
        in_specs=[SMEM, SMEM, VMEM],
        out_specs=[VMEM, VMEM, VMEM],
        out_shape=[
            jax.ShapeDtypeStruct((levels, 2 * length, length), BF16),
            jax.ShapeDtypeStruct((levels, 64, length), BF16),
            jax.ShapeDtypeStruct((128, levels * length), BF16),
        ],
        scratch_shapes=[
            pltpu.VMEM((4, 128, 128), F32),
            pltpu.VMEM((128, 128), F32),
            pltpu.VMEM((length, levels, 256), F32),
            pltpu.VMEM((length, levels, 256), F32),
        ],
        compiler_params=pltpu.CompilerParams(vmem_limit_bytes=16 * MIB),
        cost_estimate=pl.CostEstimate(flops=2_000_000_000, bytes_accessed=4 * MIB, transcendentals=0),
        name="east_matrices",
    )(place, taps, east_filter)


def north_finish(own, edges, entered, sends):
    levels = edges.shape[0]
    pairs = entered.shape[1] // 16

    def kernel(c0_ref, b_ref, z_ref, v_ref, c_hbm, c_ref, sems):
        stores = [
            pltpu.make_async_copy(
                c_ref.at[:, pl.ds(8 * j, 8)], c_hbm.at[:, pl.ds(8 * j, 8)], sems.at[j]
            )
            for j in range(levels // 2)
        ]
        empty = jnp.zeros((16, 128), BF16)
        for l in range(levels):
            values = [
                jnp.concatenate(split(z_ref[l, 16 * p : 16 * p + 16, :]), axis=1) for p in range(pairs)
            ]
            out = dot_nt(
                jnp.concatenate([v_ref[l], v_ref[l]], axis=1), jnp.concatenate(values * 2, axis=0)
            )
            high, low = split_rounded(out[0:32] + out[32:64])
            left = jnp.where(lanes_of(32) < 64, high, low).astype(BF16)
            left = jnp.concatenate([left, left], axis=1)
            blocks = [
                jnp.concatenate(
                    [
                        jnp.concatenate([piece if p == q else empty for q in range(pairs)], axis=1)
                        for p in range(pairs)
                    ],
                    axis=0,
                )
                for piece in (b_ref[l, 0:16], b_ref[l, 16:32])
            ]
            out = dot(left, jnp.concatenate([blocks[0], blocks[0], blocks[1], blocks[1]], axis=0))
            for e in range(8):
                at = slice(4 * l, 4 * l + 4)
                c_ref[e, at, :] = c0_ref[e, at, :] + out[4 * e : 4 * e + 4]
            if l % 2:
                stores[l // 2].start()
        for store in stores:
            store.wait()

    return pl.pallas_call(
        kernel,
        in_specs=[VMEM] * 4,
        out_specs=HBM,
        out_shape=jax.ShapeDtypeStruct(own.shape, F32),
        scratch_shapes=[pltpu.VMEM(own.shape, F32), pltpu.SemaphoreType.DMA((levels // 2,))],
        compiler_params=pltpu.CompilerParams(vmem_limit_bytes=16 * MIB),
        name="north_finish",
    )(own, edges, entered, sends)


def own_increment(taps, alpha, slab, columns, entered, east, perturbations, scale):
    members, levels, rows, width = alpha.shape

    def kernel(taps_ref, alpha_hbm, slab_ref, u_ref, z_ref, e_ref, pert_ref, out_ref, keep_ref, alpha_ref, s_ref, sems):
        fetches = copies(alpha_hbm, alpha_ref, sems, members)
        for fetch in fetches:
            fetch.start()
        for fetch in fetches:
            fetch.wait()
        for l in range(levels):
            added = dot(u_ref[l], edge_right(z_ref, l, members))
            for first, out in north_slab(slab_left(slab_ref[:, l, :]), alpha_ref, l, members):
                out = out + added[:, width * first : width * (first + 4)]
                field = jnp.concatenate([out[:, width * m : width * m + width] for m in range(4)], axis=0)
                high, low = split(field)
                e_high = e_ref[l, 0:width]
                s_ref[l, rows * first : rows * (first + 4)] = dot(
                    jnp.concatenate([high, low], axis=1), jnp.concatenate([e_high, e_high], axis=0)
                ) + dot(high, e_ref[l, width : 2 * width])
        tap = [taps_ref[o] * scale for o in range(5)]
        for k in range(levels):
            total = jnp.zeros((rows, width), F32)
            for m in range(members):
                mixed = sum(
                    tap[o] * s_ref[k + o - 2, rows * m : rows * m + rows, :]
                    for o in range(5)
                    if 0 <= k + o - 2 < levels
                )
                total = total + pert_ref[m, k].astype(F32) * mixed
            out_ref[k] = total
        keep_ref[...] = pert_ref[...]

    return pl.pallas_call(
        kernel,
        in_specs=[SMEM, HBM] + [VMEM] * 5,
        out_specs=[VMEM, VMEM],
        out_shape=[
            jax.ShapeDtypeStruct((levels, rows, width), F32),
            jax.ShapeDtypeStruct(perturbations.shape, BF16),
        ],
        scratch_shapes=[
            pltpu.VMEM(alpha.shape, F32),
            pltpu.VMEM((levels, members * rows, width), F32),
            pltpu.SemaphoreType.DMA((members,)),
        ],
        compiler_params=pltpu.CompilerParams(vmem_limit_bytes=51 * MIB),
        cost_estimate=pl.CostEstimate(flops=2_000_000_000, bytes_accessed=4 * MIB, transcendentals=0),
        name="own_increment",
    )(taps, alpha, slab, columns, entered, east, perturbations)


def finish(place, received, columns, perturbations, partial):
    members, levels, rows, width = perturbations.shape
    slabs = received.shape[0]

    def kernel(e_ref, r_ref, w_ref, pert_ref, part_ref, out_ref):
        me = e_ref[0]
        entering = jnp.zeros(r_ref.shape[1:], F32)
        pending = jnp.zeros(r_ref.shape[1:], F32)
        for s in range(slabs):
            block = r_ref[s]
            entering = entering + jnp.where(s < me, block, 0.0)
            pending = pending + jnp.where(s > me, block, 0.0)
        edge = jnp.concatenate([entering, pending] * 2, axis=0).T
        high, low = split_rounded(edge)
        left = jnp.where(lanes_of(members * rows) < 64, high, low).astype(BF16)
        left = jnp.concatenate([left, left], axis=1)
        for k in range(levels):
            out_ref[k] = part_ref[k]
        high, low = w_ref[0:64], w_ref[64:128]
        right = jnp.concatenate([high, high, low, low], axis=0)
        for m in range(members):
            added = dot(left[rows * m : rows * m + rows], right)
            for k in range(levels):
                out_ref[k] += pert_ref[m, k].astype(F32) * added[:, width * k : width * k + width]

    return pl.pallas_call(
        kernel,
        in_specs=[SMEM] + [VMEM] * 4,
        out_specs=VMEM,
        out_shape=jax.ShapeDtypeStruct((levels, rows, width), F32),
        compiler_params=pltpu.CompilerParams(vmem_limit_bytes=16 * MIB),
        name="finish",
    )(place, received, columns, perturbations, partial)


def local(alpha_fields, perturbations, north_filter, east_filter, depth_taps):
    members, levels, rows, width = alpha_fields.shape
    scale = 1.0 / math.sqrt(members * lax.axis_size("group") - 1)
    place = jnp.full((1,), lax.axis_index("east"), jnp.int32)
    functionals, slab = north_functionals(levels, members, rows)(north_filter, alpha_fields)
    gathered = lax.all_to_all(functionals, "north", 0, 0)
    east, sends, columns = east_matrices(place, depth_taps, east_filter, scale)
    gathered, sends = lax.optimization_barrier((gathered, sends))
    chained, slab = lax.optimization_barrier((chain_slabs(gathered), slab))
    entered = lax.all_to_all(chained, "north", 0, 0).reshape(levels, 8 * members, width)
    own, edge, blocks = own_crossing(alpha_fields, slab, sends)
    crossing = north_finish(own, blocks, entered, sends)
    crossing, entered = lax.optimization_barrier((crossing, entered))
    crossed = lax.all_to_all(crossing, "east", 0, 0)
    partial, kept = own_increment(depth_taps, alpha_fields, slab, edge, entered, east, perturbations, scale)
    increment = finish(place, crossed, columns, kept, partial)
    return increment + lax.ppermute(increment, "group", [(0, 1), (1, 0)])


def solution(mesh):
    placed = (
        P("group", None, "north", "east"),
        P("group", None, "north", "east"),
        P(None, None, "north"),
        P(),
        P(),
    )
    return jax.shard_map(
        local, mesh=mesh, in_specs=placed, out_specs=P(None, "north", "east"), check_vma=False
    )
```

```python
import math

import jax
import jax.numpy as jnp
from jax import lax
from jax.experimental import pallas as pl
from jax.experimental.pallas import tpu as pltpu
from jax.sharding import PartitionSpec as P

F32 = jnp.float32
BF16 = jnp.bfloat16
VMEM = pl.BlockSpec(memory_space=pltpu.VMEM)
SMEM = pl.BlockSpec(memory_space=pltpu.SMEM)
HBM = pl.BlockSpec(memory_space=pltpu.HBM)
MIB = 1 << 20


def split(x):
    high = x.astype(BF16)
    return high, (x - high.astype(F32)).astype(BF16)


def split_rounded(x):
    high = x.astype(BF16).astype(F32)
    return high, x - high


def dot(a, b):
    return jnp.dot(a, b, preferred_element_type=F32)


def dot_nt(a, b):
    return lax.dot_general(a, b, (((1,), (1,)), ((), ())), preferred_element_type=F32)


def wide(column, lanes=128):
    return jnp.broadcast_to(column, (column.shape[0], lanes))


def lanes_of(rows=8, lanes=128):
    return lax.broadcasted_iota(jnp.int32, (rows, lanes), 1)


def rows_of(rows=8, lanes=128):
    return lax.broadcasted_iota(jnp.int32, (rows, lanes), 0)


def copies(source, target, sems, count):
    return [pltpu.make_async_copy(source.at[i], target.at[i], sems.at[i]) for i in range(count)]


def unit(mask):
    return jnp.where(mask, 1.0, 0.0).astype(F32)


def north_functionals(levels, members, rows):
    def kernel(
        nf_hbm, alpha_hbm, p_hbm, s_hbm, nf_ref, alpha_ref, f_ref, s_ref, p_ref, w_ref, nf_sem, s_sem, sems, p_sems
    ):
        table_fetch = pltpu.make_async_copy(nf_hbm, nf_ref, nf_sem)
        table_fetch.start()
        fetches = copies(alpha_hbm, alpha_ref, sems, members)
        stores = copies(p_ref, p_hbm, p_sems, 2 * levels)
        slab_store = pltpu.make_async_copy(s_ref, s_hbm, s_sem)
        for fetch in fetches:
            fetch.start()
        table_fetch.wait()
        lane = lanes_of()
        table = [nf_ref[j] for j in range(5)]
        gain = jnp.concatenate([jnp.zeros((levels, 64), F32), table[0]], axis=1)
        state = [unit(lane == k) for k in range(4)]
        for i in range(rows):
            value = jnp.where(lane == 64 + i, gain, 0.0)
            for j in (4, 3, 2, 1):
                weight = wide(table[j][:, i : i + 1])
                w_ref[i, j - 1] = weight
                value = value + weight * state[j - 1]
            f_ref[i] = value + unit(lane == 4 + rows - 1 - i) if i >= rows - 4 else value
            state = [value] + state[:3]
        state = [jnp.zeros((levels, 128), F32)] * 4
        for i in reversed(range(rows)):
            value = f_ref[i]
            for j in (4, 3, 2, 1):
                if i + j < rows:
                    value = value + w_ref[i + j, j - 1] * state[j - 1]
            s_ref[i] = value * wide(table[0][:, i : i + 1])
            state = [value] + state[:3]
        slab_store.start()
        lefts = []
        for l in range(levels):
            flat = f_ref[:, l, :]
            maps = jnp.dot(
                flat.T[0:8], flat, precision=lax.Precision.HIGHEST, preferred_element_type=F32
            )
            p_ref[2 * l, 32:40, :] = maps
            p_ref[2 * l + 1, 32:40, :] = maps
            edge = s_ref[:, l, :].T[0:8]
            high, low = split_rounded(jnp.concatenate([edge, edge], axis=1))
            lefts.append(jnp.concatenate([high, low], axis=0).astype(BF16))
        for fetch in fetches:
            fetch.wait()
        for l in range(levels):
            for half in range(2):
                right = []
                for m in range(4):
                    a_high, a_low = split(alpha_ref[half * 4 + m, l])
                    right.append(jnp.concatenate([a_high, a_low], axis=0))
                out = dot(lefts[l], jnp.concatenate(right, axis=1))
                out = out[0:8] + out[8:16]
                for m in range(4):
                    p_ref[2 * l + half, 8 * m : 8 * m + 8, :] = out[:, 128 * m : 128 * m + 128]
                stores[2 * l + half].start()
        for store in stores + [slab_store]:
            store.wait()

    def call(north_filter, alpha):
        return pl.pallas_call(
            kernel,
            in_specs=[HBM, HBM],
            out_specs=[HBM, HBM],
            out_shape=[
                jax.ShapeDtypeStruct((2 * levels, 40, 128), F32),
                jax.ShapeDtypeStruct((rows, levels, 128), F32),
            ],
            scratch_shapes=[
                pltpu.VMEM(north_filter.shape, F32),
                pltpu.VMEM(alpha.shape, F32),
                pltpu.VMEM((rows, levels, 128), F32),
                pltpu.VMEM((rows, levels, 128), F32),
                pltpu.VMEM((2 * levels, 40, 128), F32),
                pltpu.VMEM((rows, 4, levels, 128), F32),
                pltpu.SemaphoreType.DMA,
                pltpu.SemaphoreType.DMA,
                pltpu.SemaphoreType.DMA((members,)),
                pltpu.SemaphoreType.DMA((2 * levels,)),
            ],
            compiler_params=pltpu.CompilerParams(vmem_limit_bytes=63 * MIB),
            name="north_functionals",
        )(north_filter, alpha)

    return call


def chain_slabs(received):
    slabs = received.shape[0]

    def kernel(r_ref, z_ref, v_ref):
        state = [jnp.zeros((4, 128), F32)] * 4
        for n in range(slabs):
            maps = r_ref[n, 32:40, :]
            column = [wide(maps[:, j : j + 1]) for j in range(4)]
            for m in range(4):
                z_ref[n, 8 * m : 8 * m + 4, :] = state[m]
                value = r_ref[n, 8 * m : 8 * m + 8, :]
                for j in range(4):
                    value = value + column[j] * jnp.broadcast_to(state[m][j : j + 1], (8, 128))
                v_ref[n, 4 * m : 4 * m + 4, :] = value[0:4]
                state[m] = value[4:8]
        pending = [jnp.zeros((4, 128), F32)] * 4
        for n in reversed(range(slabs)):
            maps = r_ref[n, 32:36, :]
            column = [wide(maps[:, 4 + j : 5 + j]) for j in range(4)]
            for m in range(4):
                z_ref[n, 8 * m + 4 : 8 * m + 8, :] = pending[m]
                value = v_ref[n, 4 * m : 4 * m + 4, :]
                for j in range(4):
                    value = value + column[j] * jnp.broadcast_to(pending[m][j : j + 1], (4, 128))
                pending[m] = value

    return pl.pallas_call(
        kernel,
        in_specs=[VMEM],
        out_specs=VMEM,
        out_shape=jax.ShapeDtypeStruct((slabs, 32, 128), F32),
        scratch_shapes=[pltpu.VMEM((slabs, 16, 128), F32)],
        compiler_params=pltpu.CompilerParams(vmem_limit_bytes=8 * MIB),
        name="chain_slabs",
    )(received)


def north_slab(left, alpha_ref, l, members):
    for first in range(0, members, 4):
        right = []
        for m in range(first, first + 4):
            high, low = split(alpha_ref[m, l])
            right.append(jnp.concatenate([high, low, high, low], axis=0))
        yield first, dot(left, jnp.concatenate(right, axis=1))


def slab_left(full):
    twice = jnp.where(lanes_of(full.shape[0]) < 64, pltpu.roll(full, 64, 1), full)
    high, low = split(twice)
    return jnp.concatenate([high, low], axis=1)


def edge_right(z_ref, l, members):
    right = []
    for m in range(members):
        high, low = split_rounded(z_ref[l, 8 * m : 8 * m + 8, :])
        right.append(jnp.concatenate([high, low, high, low], axis=0).astype(BF16))
    return jnp.concatenate(right, axis=1)


def crossing_rows(v_ref, l, fields):
    parts = jnp.concatenate([jnp.concatenate(split(field), axis=1) for field in fields], axis=0)
    out = dot_nt(jnp.concatenate([v_ref[l], v_ref[l]], axis=1), parts)
    return out[0:32] + out[32:64]


def own_crossing(alpha, slab, sends):
    members, levels, rows, width = alpha.shape

    def kernel(alpha_hbm, s_ref, v_ref, c_ref, u_ref, b_ref, alpha_ref, sems):
        fetches = copies(alpha_hbm, alpha_ref, sems, members)
        for fetch in fetches:
            fetch.start()
        for fetch in fetches:
            fetch.wait()
        lane = lanes_of()
        for l in range(levels):
            full = s_ref[:, l, :]
            fields = []
            for _, out in north_slab(slab_left(full), alpha_ref, l, members):
                fields += [out[:, width * m : width * m + width] for m in range(4)]
            out = crossing_rows(v_ref, l, fields)
            for e in range(8):
                c_ref[e, 4 * l : 4 * l + 4, :] = out[4 * e : 4 * e + 4]
            high, low = split_rounded(full[:, 0:8])
            u_ref[l] = jnp.concatenate([high, high, low, low], axis=1).astype(BF16)
            edge = full.T[0:8]
            edge = jnp.concatenate([edge, edge], axis=1)
            edge = jnp.concatenate([jnp.where(lane < 64, edge, 0.0), jnp.where(lane < 64, 0.0, edge)], axis=0)
            b_ref[l] = jnp.concatenate(split(edge), axis=0)

    return pl.pallas_call(
        kernel,
        in_specs=[HBM, VMEM, VMEM],
        out_specs=[VMEM] * 3,
        scratch_shapes=[pltpu.VMEM(alpha.shape, F32), pltpu.SemaphoreType.DMA((members,))],
        out_shape=[
            jax.ShapeDtypeStruct((8, 4 * levels, members * rows), F32),
            jax.ShapeDtypeStruct((levels, rows, 32), BF16),
            jax.ShapeDtypeStruct((levels, 32, 128), BF16),
        ],
        compiler_params=pltpu.CompilerParams(vmem_limit_bytes=51 * MIB),
        cost_estimate=pl.CostEstimate(flops=2_000_000_000, bytes_accessed=4 * MIB, transcendentals=0),
        name="own_crossing",
    )(alpha, slab, sends)


def east_matrices(place, taps, east_filter, scale):
    levels = east_filter.shape[1]
    length = 128
    slabs = east_filter.shape[2] // length

    def kernel(e_ref, taps_ref, ef_ref, e_out, v_out, w_out, wt_ref, rt_ref, f_ref, s_ref, near_ref):
        me = e_ref[0]
        lane = lanes_of()
        row = rows_of()
        for j in range(1, 5):
            stacked = jnp.concatenate(
                [ef_ref[j, :, length * s : length * (s + 1)] for s in range(slabs)] * 2, axis=0
            )
            wt_ref[j - 1] = stacked.T
        state = [unit(row == k) for k in range(4)]
        gram = [jnp.zeros((8, 128), F32)] * 4
        for i in range(length):
            value = jnp.zeros((8, 128), F32)
            for j in (3, 2, 1, 0):
                value = value + jnp.broadcast_to(wt_ref[j, i : i + 1, :], (8, 128)) * state[j]
            gram = [gram[k] + value * jnp.broadcast_to(value[k : k + 1], (8, 128)) for k in range(4)]
            state = [value] + state[:3]
        step = state
        reflect = [jnp.zeros((8, 128), F32)] * 4
        for _ in range(slabs - 1):
            inner = [
                sum(jnp.broadcast_to(reflect[i][j : j + 1], (8, 128)) * step[j] for j in range(4))
                for i in range(4)
            ]
            outer = [
                gram[a]
                + sum(jnp.broadcast_to(step[i][a : a + 1], (8, 128)) * inner[i] for i in range(4))
                for a in range(4)
            ]
            reflect = [jnp.where(lane < 56, pltpu.roll(outer[a], 120, 1), 0.0) for a in range(4)]
        rt_ref[...] = jnp.concatenate(reflect * 4, axis=0).T
        back = rt_ref[pl.ds(pl.multiple_of(me * 8, 8), 8), :]
        own = [ef_ref[j, :, pl.ds(pl.multiple_of(me * length, length), length)] for j in range(5)]
        core = [jnp.zeros((levels, 128), F32)] * 4
        side = [unit(lane == k) for k in range(4)]
        for i in range(length):
            weight = [wide(own[j][:, i : i + 1]) for j in range(1, 5)]
            for j in range(4):
                near_ref[i, j] = weight[j]
            c_value = jnp.where(lane == i, own[0], 0.0)
            s_value = jnp.zeros((levels, 128), F32)
            for j in (3, 2, 1, 0):
                c_value = c_value + weight[j] * core[j]
                s_value = s_value + weight[j] * side[j]
            f_ref[i, :, 0:128] = c_value
            f_ref[i, :, 128:256] = s_value
            core = [c_value] + core[:3]
            side = [s_value] + side[:3]
        for k in range(4):
            c_value, s_value = core[k], side[k]
            for j in range(4):
                weight = wide(back[:, 8 * k + j : 8 * k + j + 1])
                c_value = c_value + weight * core[j]
                s_value = s_value + weight * side[j]
            f_ref[length - 1 - k, :, 0:128] = c_value
            f_ref[length - 1 - k, :, 128:256] = s_value + unit(lane == 4 + k)
        core = [jnp.zeros((levels, 128), F32)] * 4
        side = [jnp.zeros((levels, 128), F32)] * 4
        for i in reversed(range(length)):
            c_value = f_ref[i, :, 0:128]
            s_value = f_ref[i, :, 128:256]
            for j in (4, 3, 2, 1):
                if i + j < length:
                    weight = near_ref[i + j, j - 1]
                    c_value = c_value + weight * core[j - 1]
                    s_value = s_value + weight * side[j - 1]
            gain = wide(own[0][:, i : i + 1])
            s_ref[i, :, 0:128] = c_value * gain
            s_ref[i, :, 128:256] = s_value * gain
            core = [c_value] + core[:3]
            side = [s_value] + side[:3]
        across = [
            jnp.concatenate([step[i][j : j + 1] for i in range(4)], axis=0) for j in range(4)
        ]
        entering, pending = [], []
        for l in range(levels):
            e_out[l] = jnp.concatenate(split(s_ref[:, l, 0:128]), axis=0)
            edge = s_ref[:, l, 128:256].T[0:8]
            entering.append(edge[0:4])
            pending.append(edge[4:8])
        upward, downward = [pending], [entering]
        for e in range(1, slabs):
            for chain, column, at, beyond, first in (
                (upward, across, e - 1, e - 1 > me, pending),
                (downward, step, slabs - e, slabs - e < me, entering),
            ):
                moved = [
                    sum(
                        wide(column[j][0:4, 8 * at + l : 8 * at + l + 1])
                        * jnp.broadcast_to(chain[-1][l][j : j + 1], (4, 128))
                        for j in range(4)
                    )
                    for l in range(levels)
                ]
                chain.append([jnp.where(beyond, moved[l], first[l]) for l in range(levels)])
        downward.reverse()
        for l in range(levels):
            sends = jnp.concatenate(
                [jnp.where(e > me, upward[e][l], downward[e][l]) for e in range(slabs)], axis=0
            )
            v_out[l] = jnp.concatenate(split_rounded(sends), axis=0).astype(BF16)
        columns = jnp.concatenate(entering + pending, axis=0)
        level = lax.rem(rows_of(64), 32) // 4
        for k in range(levels):
            mix = jnp.zeros((64, 128), F32)
            for offset in range(5):
                mix = mix + jnp.where(level - k == offset - 2, taps_ref[offset] * scale, 0.0)
            high, low = split(columns * mix)
            w_out[:, 128 * k : 128 * k + 128] = jnp.concatenate([high, low], axis=0)

    return pl.pallas_call(
        kernel,
        in_specs=[SMEM, SMEM, VMEM],
        out_specs=[VMEM, VMEM, VMEM],
        out_shape=[
            jax.ShapeDtypeStruct((levels, 2 * length, length), BF16),
            jax.ShapeDtypeStruct((levels, 64, length), BF16),
            jax.ShapeDtypeStruct((128, levels * length), BF16),
        ],
        scratch_shapes=[
            pltpu.VMEM((4, 128, 128), F32),
            pltpu.VMEM((128, 128), F32),
            pltpu.VMEM((length, levels, 256), F32),
            pltpu.VMEM((length, levels, 256), F32),
            pltpu.VMEM((length, 4, levels, 128), F32),
        ],
        compiler_params=pltpu.CompilerParams(vmem_limit_bytes=16 * MIB),
        cost_estimate=pl.CostEstimate(flops=2_000_000_000, bytes_accessed=4 * MIB, transcendentals=0),
        name="east_matrices",
    )(place, taps, east_filter)


def north_finish(own, edges, entered, sends):
    levels = edges.shape[0]
    pairs = entered.shape[1] // 16

    def kernel(c0_ref, b_ref, z_ref, v_ref, c_hbm, c_ref, sems):
        stores = [
            pltpu.make_async_copy(
                c_ref.at[:, pl.ds(8 * j, 8)], c_hbm.at[:, pl.ds(8 * j, 8)], sems.at[j]
            )
            for j in range(levels // 2)
        ]
        empty = jnp.zeros((16, 128), BF16)
        lefts = []
        for l in range(levels):
            values = [
                jnp.concatenate(split(z_ref[l, 16 * p : 16 * p + 16, :]), axis=1) for p in range(pairs)
            ]
            out = dot_nt(
                jnp.concatenate([v_ref[l], v_ref[l]], axis=1), jnp.concatenate(values * 2, axis=0)
            )
            high, low = split_rounded(out[0:32] + out[32:64])
            left = jnp.where(lanes_of(32) < 64, high, low).astype(BF16)
            lefts.append(jnp.concatenate([left, left], axis=1))
        for l in range(levels):
            blocks = [
                jnp.concatenate(
                    [
                        jnp.concatenate([piece if p == q else empty for q in range(pairs)], axis=1)
                        for p in range(pairs)
                    ],
                    axis=0,
                )
                for piece in (b_ref[l, 0:16], b_ref[l, 16:32])
            ]
            out = dot(lefts[l], jnp.concatenate([blocks[0], blocks[0], blocks[1], blocks[1]], axis=0))
            for e in range(8):
                at = slice(4 * l, 4 * l + 4)
                c_ref[e, at, :] = c0_ref[e, at, :] + out[4 * e : 4 * e + 4]
            if l % 2:
                stores[l // 2].start()
        for store in stores:
            store.wait()

    return pl.pallas_call(
        kernel,
        in_specs=[VMEM] * 4,
        out_specs=HBM,
        out_shape=jax.ShapeDtypeStruct(own.shape, F32),
        scratch_shapes=[pltpu.VMEM(own.shape, F32), pltpu.SemaphoreType.DMA((levels // 2,))],
        compiler_params=pltpu.CompilerParams(vmem_limit_bytes=16 * MIB),
        name="north_finish",
    )(own, edges, entered, sends)


def own_increment(taps, alpha, slab, columns, entered, east, perturbations, scale):
    members, levels, rows, width = alpha.shape

    def kernel(taps_ref, alpha_hbm, slab_ref, u_ref, z_ref, e_ref, pert_ref, out_ref, keep_ref, alpha_ref, s_ref, sems):
        fetches = copies(alpha_hbm, alpha_ref, sems, members)
        for fetch in fetches:
            fetch.start()
        for fetch in fetches:
            fetch.wait()
        for l in range(levels):
            added = dot(u_ref[l], edge_right(z_ref, l, members))
            for first, out in north_slab(slab_left(slab_ref[:, l, :]), alpha_ref, l, members):
                out = out + added[:, width * first : width * (first + 4)]
                field = jnp.concatenate([out[:, width * m : width * m + width] for m in range(4)], axis=0)
                high, low = split(field)
                e_high = e_ref[l, 0:width]
                s_ref[l, rows * first : rows * (first + 4)] = dot(
                    jnp.concatenate([high, low], axis=1), jnp.concatenate([e_high, e_high], axis=0)
                ) + dot(high, e_ref[l, width : 2 * width])
        tap = [taps_ref[o] * scale for o in range(5)]
        for k in range(levels):
            total = jnp.zeros((rows, width), F32)
            for m in range(members):
                mixed = sum(
                    tap[o] * s_ref[k + o - 2, rows * m : rows * m + rows, :]
                    for o in range(5)
                    if 0 <= k + o - 2 < levels
                )
                total = total + pert_ref[m, k].astype(F32) * mixed
            out_ref[k] = total
        keep_ref[...] = pert_ref[...]

    return pl.pallas_call(
        kernel,
        in_specs=[SMEM, HBM] + [VMEM] * 5,
        out_specs=[VMEM, VMEM],
        out_shape=[
            jax.ShapeDtypeStruct((levels, rows, width), F32),
            jax.ShapeDtypeStruct(perturbations.shape, BF16),
        ],
        scratch_shapes=[
            pltpu.VMEM(alpha.shape, F32),
            pltpu.VMEM((levels, members * rows, width), F32),
            pltpu.SemaphoreType.DMA((members,)),
        ],
        compiler_params=pltpu.CompilerParams(vmem_limit_bytes=51 * MIB),
        cost_estimate=pl.CostEstimate(flops=2_000_000_000, bytes_accessed=4 * MIB, transcendentals=0),
        name="own_increment",
    )(taps, alpha, slab, columns, entered, east, perturbations)


def finish(place, received, columns, perturbations, partial):
    members, levels, rows, width = perturbations.shape
    slabs = received.shape[0]

    def kernel(e_ref, r_ref, w_ref, pert_ref, part_ref, out_ref):
        me = e_ref[0]
        entering = jnp.zeros(r_ref.shape[1:], F32)
        pending = jnp.zeros(r_ref.shape[1:], F32)
        for s in range(slabs):
            block = r_ref[s]
            entering = entering + jnp.where(s < me, block, 0.0)
            pending = pending + jnp.where(s > me, block, 0.0)
        edge = jnp.concatenate([entering, pending] * 2, axis=0).T
        high, low = split_rounded(edge)
        left = jnp.where(lanes_of(members * rows) < 64, high, low).astype(BF16)
        left = jnp.concatenate([left, left], axis=1)
        for k in range(levels):
            out_ref[k] = part_ref[k]
        high, low = w_ref[0:64], w_ref[64:128]
        right = jnp.concatenate([high, high, low, low], axis=0)
        for m in range(members):
            added = dot(left[rows * m : rows * m + rows], right)
            for k in range(levels):
                out_ref[k] += pert_ref[m, k].astype(F32) * added[:, width * k : width * k + width]

    return pl.pallas_call(
        kernel,
        in_specs=[SMEM] + [VMEM] * 4,
        out_specs=VMEM,
        out_shape=jax.ShapeDtypeStruct((levels, rows, width), F32),
        compiler_params=pltpu.CompilerParams(vmem_limit_bytes=16 * MIB),
        name="finish",
    )(place, received, columns, perturbations, partial)


def local(alpha_fields, perturbations, north_filter, east_filter, depth_taps):
    members, levels, rows, width = alpha_fields.shape
    scale = 1.0 / math.sqrt(members * lax.axis_size("group") - 1)
    place = jnp.full((1,), lax.axis_index("east"), jnp.int32)
    functionals, slab = north_functionals(levels, members, rows)(north_filter, alpha_fields)
    gathered = lax.all_to_all(functionals, "north", 0, 0)
    east, sends, columns = east_matrices(place, depth_taps, east_filter, scale)
    gathered, sends = lax.optimization_barrier((gathered, sends))
    chained, slab = lax.optimization_barrier((chain_slabs(gathered), slab))
    entered = lax.all_to_all(chained, "north", 0, 0).reshape(levels, 8 * members, width)
    own, edge, blocks = own_crossing(alpha_fields, slab, sends)
    crossing = north_finish(own, blocks, entered, sends)
    crossing, entered = lax.optimization_barrier((crossing, entered))
    crossed = lax.all_to_all(crossing, "east", 0, 0)
    partial, kept = own_increment(depth_taps, alpha_fields, slab, edge, entered, east, perturbations, scale)
    increment = finish(place, crossed, columns, kept, partial)
    return increment + lax.ppermute(increment, "group", [(0, 1), (1, 0)])


def solution(mesh):
    placed = (
        P("group", None, "north", "east"),
        P("group", None, "north", "east"),
        P(None, None, "north"),
        P(),
        P(),
    )
    return jax.shard_map(
        local, mesh=mesh, in_specs=placed, out_specs=P(None, "north", "east"), check_vma=False
    )
```

```python
import math

import jax
import jax.numpy as jnp
from jax import lax
from jax.experimental import pallas as pl
from jax.experimental.pallas import tpu as pltpu
from jax.sharding import PartitionSpec as P

F32 = jnp.float32
BF16 = jnp.bfloat16
VMEM = pl.BlockSpec(memory_space=pltpu.VMEM)
SMEM = pl.BlockSpec(memory_space=pltpu.SMEM)
HBM = pl.BlockSpec(memory_space=pltpu.HBM)
MIB = 1 << 20


def split(x):
    high = x.astype(BF16)
    return high, (x - high.astype(F32)).astype(BF16)


def split_rounded(x):
    high = x.astype(BF16).astype(F32)
    return high, x - high


def dot(a, b):
    return jnp.dot(a, b, preferred_element_type=F32)


def dot_nt(a, b):
    return lax.dot_general(a, b, (((1,), (1,)), ((), ())), preferred_element_type=F32)


def wide(column, lanes=128):
    return jnp.broadcast_to(column, (column.shape[0], lanes))


def lanes_of(rows=8, lanes=128):
    return lax.broadcasted_iota(jnp.int32, (rows, lanes), 1)


def rows_of(rows=8, lanes=128):
    return lax.broadcasted_iota(jnp.int32, (rows, lanes), 0)


def copies(source, target, sems, count):
    return [pltpu.make_async_copy(source.at[i], target.at[i], sems.at[i]) for i in range(count)]


def unit(mask):
    return jnp.where(mask, 1.0, 0.0).astype(F32)


def north_functionals(levels, members, rows):
    def kernel(
        nf_hbm, alpha_hbm, p_hbm, s_hbm, nf_ref, alpha_ref, f_ref, s_ref, p_ref, w_ref, nf_sem, s_sem, sem, p_sems
    ):
        table_fetch = pltpu.make_async_copy(nf_hbm, nf_ref, nf_sem)
        table_fetch.start()
        fetch = pltpu.make_async_copy(alpha_hbm, alpha_ref, sem)
        stores = copies(p_ref, p_hbm, p_sems, 2 * levels)
        slab_store = pltpu.make_async_copy(s_ref, s_hbm, s_sem)
        fetch.start()
        table_fetch.wait()
        lane = lanes_of()
        table = [nf_ref[j] for j in range(5)]
        gain = jnp.concatenate([jnp.zeros((levels, 64), F32), table[0]], axis=1)
        state = [unit(lane == k) for k in range(4)]
        for i in range(rows):
            value = jnp.where(lane == 64 + i, gain, 0.0)
            for j in (4, 3, 2, 1):
                weight = wide(table[j][:, i : i + 1])
                w_ref[i, j - 1] = weight
                value = value + weight * state[j - 1]
            f_ref[i] = value + unit(lane == 4 + rows - 1 - i) if i >= rows - 4 else value
            state = [value] + state[:3]
        state = [jnp.zeros((levels, 128), F32)] * 4
        for i in reversed(range(rows)):
            value = f_ref[i]
            for j in (4, 3, 2, 1):
                if i + j < rows:
                    value = value + w_ref[i + j, j - 1] * state[j - 1]
            s_ref[i] = value * wide(table[0][:, i : i + 1])
            state = [value] + state[:3]
        slab_store.start()
        lefts = []
        for l in range(levels):
            flat = f_ref[:, l, :]
            maps = jnp.dot(
                flat.T[0:8], flat, precision=lax.Precision.HIGHEST, preferred_element_type=F32
            )
            p_ref[2 * l, 32:40, :] = maps
            p_ref[2 * l + 1, 32:40, :] = maps
            edge = s_ref[:, l, :].T[0:8]
            high, low = split_rounded(jnp.concatenate([edge, edge], axis=1))
            lefts.append(jnp.concatenate([high, low], axis=0).astype(BF16))
        fetch.wait()
        for l in range(levels):
            for half in range(2):
                right = []
                for m in range(4):
                    a_high, a_low = split(alpha_ref[half * 4 + m, l])
                    right.append(jnp.concatenate([a_high, a_low], axis=0))
                out = dot(lefts[l], jnp.concatenate(right, axis=1))
                out = out[0:8] + out[8:16]
                for m in range(4):
                    p_ref[2 * l + half, 8 * m : 8 * m + 8, :] = out[:, 128 * m : 128 * m + 128]
                stores[2 * l + half].start()
        for store in stores + [slab_store]:
            store.wait()

    def call(north_filter, alpha):
        return pl.pallas_call(
            kernel,
            in_specs=[HBM, HBM],
            out_specs=[HBM, HBM],
            out_shape=[
                jax.ShapeDtypeStruct((2 * levels, 40, 128), F32),
                jax.ShapeDtypeStruct((rows, levels, 128), F32),
            ],
            scratch_shapes=[
                pltpu.VMEM(north_filter.shape, F32),
                pltpu.VMEM(alpha.shape, F32),
                pltpu.VMEM((rows, levels, 128), F32),
                pltpu.VMEM((rows, levels, 128), F32),
                pltpu.VMEM((2 * levels, 40, 128), F32),
                pltpu.VMEM((rows, 4, levels, 128), F32),
                pltpu.SemaphoreType.DMA,
                pltpu.SemaphoreType.DMA,
                pltpu.SemaphoreType.DMA,
                pltpu.SemaphoreType.DMA((2 * levels,)),
            ],
            compiler_params=pltpu.CompilerParams(vmem_limit_bytes=63 * MIB),
            name="north_functionals",
        )(north_filter, alpha)

    return call


def chain_slabs(received):
    slabs = received.shape[0]

    def kernel(r_ref, z_ref, v_ref):
        state = [jnp.zeros((4, 128), F32)] * 4
        for n in range(slabs):
            maps = r_ref[n, 32:40, :]
            column = [wide(maps[:, j : j + 1]) for j in range(4)]
            for m in range(4):
                z_ref[n, 8 * m : 8 * m + 4, :] = state[m]
                value = r_ref[n, 8 * m : 8 * m + 8, :]
                for j in range(4):
                    value = value + column[j] * jnp.broadcast_to(state[m][j : j + 1], (8, 128))
                v_ref[n, 4 * m : 4 * m + 4, :] = value[0:4]
                state[m] = value[4:8]
        pending = [jnp.zeros((4, 128), F32)] * 4
        for n in reversed(range(slabs)):
            maps = r_ref[n, 32:36, :]
            column = [wide(maps[:, 4 + j : 5 + j]) for j in range(4)]
            for m in range(4):
                z_ref[n, 8 * m + 4 : 8 * m + 8, :] = pending[m]
                value = v_ref[n, 4 * m : 4 * m + 4, :]
                for j in range(4):
                    value = value + column[j] * jnp.broadcast_to(pending[m][j : j + 1], (4, 128))
                pending[m] = value

    return pl.pallas_call(
        kernel,
        in_specs=[VMEM],
        out_specs=VMEM,
        out_shape=jax.ShapeDtypeStruct((slabs, 32, 128), F32),
        scratch_shapes=[pltpu.VMEM((slabs, 16, 128), F32)],
        compiler_params=pltpu.CompilerParams(vmem_limit_bytes=8 * MIB),
        name="chain_slabs",
    )(received)


def north_slab(left, alpha_ref, l, members):
    for first in range(0, members, 4):
        right = []
        for m in range(first, first + 4):
            high, low = split(alpha_ref[m, l])
            right.append(jnp.concatenate([high, low, high, low], axis=0))
        yield first, dot(left, jnp.concatenate(right, axis=1))


def slab_left(full):
    twice = jnp.where(lanes_of(full.shape[0]) < 64, pltpu.roll(full, 64, 1), full)
    high, low = split(twice)
    return jnp.concatenate([high, low], axis=1)


def edge_right(z_ref, l, members):
    right = []
    for m in range(members):
        high, low = split_rounded(z_ref[l, 8 * m : 8 * m + 8, :])
        right.append(jnp.concatenate([high, low, high, low], axis=0).astype(BF16))
    return jnp.concatenate(right, axis=1)


def crossing_rows(v_ref, l, fields):
    parts = jnp.concatenate([jnp.concatenate(split(field), axis=1) for field in fields], axis=0)
    out = dot_nt(jnp.concatenate([v_ref[l], v_ref[l]], axis=1), parts)
    return out[0:32] + out[32:64]


def own_crossing(alpha, slab, sends):
    members, levels, rows, width = alpha.shape

    def kernel(alpha_hbm, s_ref, v_ref, c_ref, u_ref, b_ref, alpha_ref, sem):
        fetch = pltpu.make_async_copy(alpha_hbm, alpha_ref, sem)
        fetch.start()
        fetch.wait()
        lane = lanes_of()
        for l in range(levels):
            full = s_ref[:, l, :]
            fields = []
            for _, out in north_slab(slab_left(full), alpha_ref, l, members):
                fields += [out[:, width * m : width * m + width] for m in range(4)]
            out = crossing_rows(v_ref, l, fields)
            for e in range(8):
                c_ref[e, 4 * l : 4 * l + 4, :] = out[4 * e : 4 * e + 4]
            high, low = split_rounded(full[:, 0:8])
            u_ref[l] = jnp.concatenate([high, high, low, low], axis=1).astype(BF16)
            edge = full.T[0:8]
            edge = jnp.concatenate([edge, edge], axis=1)
            edge = jnp.concatenate([jnp.where(lane < 64, edge, 0.0), jnp.where(lane < 64, 0.0, edge)], axis=0)
            b_ref[l] = jnp.concatenate(split(edge), axis=0)

    return pl.pallas_call(
        kernel,
        in_specs=[HBM, VMEM, VMEM],
        out_specs=[VMEM] * 3,
        scratch_shapes=[pltpu.VMEM(alpha.shape, F32), pltpu.SemaphoreType.DMA],
        out_shape=[
            jax.ShapeDtypeStruct((8, 4 * levels, members * rows), F32),
            jax.ShapeDtypeStruct((levels, rows, 32), BF16),
            jax.ShapeDtypeStruct((levels, 32, 128), BF16),
        ],
        compiler_params=pltpu.CompilerParams(vmem_limit_bytes=51 * MIB),
        cost_estimate=pl.CostEstimate(flops=2_000_000_000, bytes_accessed=4 * MIB, transcendentals=0),
        name="own_crossing",
    )(alpha, slab, sends)


def east_matrices(place, taps, east_filter, scale):
    levels = east_filter.shape[1]
    length = 128
    slabs = east_filter.shape[2] // length

    def kernel(e_ref, taps_ref, ef_ref, e_out, v_out, w_out, wt_ref, rt_ref, f_ref, s_ref, near_ref):
        me = e_ref[0]
        lane = lanes_of()
        row = rows_of()
        for j in range(1, 5):
            stacked = jnp.concatenate(
                [ef_ref[j, :, length * s : length * (s + 1)] for s in range(slabs)] * 2, axis=0
            )
            wt_ref[j - 1] = stacked.T
        state = [unit(row == k) for k in range(4)]
        gram = [jnp.zeros((8, 128), F32)] * 4
        for i in range(length):
            value = jnp.zeros((8, 128), F32)
            for j in (3, 2, 1, 0):
                value = value + jnp.broadcast_to(wt_ref[j, i : i + 1, :], (8, 128)) * state[j]
            gram = [gram[k] + value * jnp.broadcast_to(value[k : k + 1], (8, 128)) for k in range(4)]
            state = [value] + state[:3]
        step = state
        reflect = [jnp.zeros((8, 128), F32)] * 4
        for _ in range(slabs - 1):
            inner = [
                sum(jnp.broadcast_to(reflect[i][j : j + 1], (8, 128)) * step[j] for j in range(4))
                for i in range(4)
            ]
            outer = [
                gram[a]
                + sum(jnp.broadcast_to(step[i][a : a + 1], (8, 128)) * inner[i] for i in range(4))
                for a in range(4)
            ]
            reflect = [jnp.where(lane < 56, pltpu.roll(outer[a], 120, 1), 0.0) for a in range(4)]
        rt_ref[...] = jnp.concatenate(reflect * 4, axis=0).T
        back = rt_ref[pl.ds(pl.multiple_of(me * 8, 8), 8), :]
        own = [ef_ref[j, :, pl.ds(pl.multiple_of(me * length, length), length)] for j in range(5)]
        core = [jnp.zeros((levels, 128), F32)] * 4
        side = [unit(lane == k) for k in range(4)]
        for i in range(length):
            weight = [wide(own[j][:, i : i + 1]) for j in range(1, 5)]
            for j in range(4):
                near_ref[i, j] = weight[j]
            c_value = jnp.where(lane == i, own[0], 0.0)
            s_value = jnp.zeros((levels, 128), F32)
            for j in (3, 2, 1, 0):
                c_value = c_value + weight[j] * core[j]
                s_value = s_value + weight[j] * side[j]
            f_ref[i, :, 0:128] = c_value
            f_ref[i, :, 128:256] = s_value
            core = [c_value] + core[:3]
            side = [s_value] + side[:3]
        for k in range(4):
            c_value, s_value = core[k], side[k]
            for j in range(4):
                weight = wide(back[:, 8 * k + j : 8 * k + j + 1])
                c_value = c_value + weight * core[j]
                s_value = s_value + weight * side[j]
            f_ref[length - 1 - k, :, 0:128] = c_value
            f_ref[length - 1 - k, :, 128:256] = s_value + unit(lane == 4 + k)
        core = [jnp.zeros((levels, 128), F32)] * 4
        side = [jnp.zeros((levels, 128), F32)] * 4
        for i in reversed(range(length)):
            c_value = f_ref[i, :, 0:128]
            s_value = f_ref[i, :, 128:256]
            for j in (4, 3, 2, 1):
                if i + j < length:
                    weight = near_ref[i + j, j - 1]
                    c_value = c_value + weight * core[j - 1]
                    s_value = s_value + weight * side[j - 1]
            gain = wide(own[0][:, i : i + 1])
            s_ref[i, :, 0:128] = c_value * gain
            s_ref[i, :, 128:256] = s_value * gain
            core = [c_value] + core[:3]
            side = [s_value] + side[:3]
        across = [
            jnp.concatenate([step[i][j : j + 1] for i in range(4)], axis=0) for j in range(4)
        ]
        entering, pending = [], []
        for l in range(levels):
            e_out[l] = jnp.concatenate(split(s_ref[:, l, 0:128]), axis=0)
            edge = s_ref[:, l, 128:256].T[0:8]
            entering.append(edge[0:4])
            pending.append(edge[4:8])
        upward, downward = [pending], [entering]
        for e in range(1, slabs):
            for chain, column, at, beyond, first in (
                (upward, across, e - 1, e - 1 > me, pending),
                (downward, step, slabs - e, slabs - e < me, entering),
            ):
                moved = [
                    sum(
                        wide(column[j][0:4, 8 * at + l : 8 * at + l + 1])
                        * jnp.broadcast_to(chain[-1][l][j : j + 1], (4, 128))
                        for j in range(4)
                    )
                    for l in range(levels)
                ]
                chain.append([jnp.where(beyond, moved[l], first[l]) for l in range(levels)])
        downward.reverse()
        for l in range(levels):
            sends = jnp.concatenate(
                [jnp.where(e > me, upward[e][l], downward[e][l]) for e in range(slabs)], axis=0
            )
            v_out[l] = jnp.concatenate(split_rounded(sends), axis=0).astype(BF16)
        columns = jnp.concatenate(entering + pending, axis=0)
        level = lax.rem(rows_of(64), 32) // 4
        for k in range(levels):
            mix = jnp.zeros((64, 128), F32)
            for offset in range(5):
                mix = mix + jnp.where(level - k == offset - 2, taps_ref[offset] * scale, 0.0)
            high, low = split(columns * mix)
            w_out[:, 128 * k : 128 * k + 128] = jnp.concatenate([high, low], axis=0)

    return pl.pallas_call(
        kernel,
        in_specs=[SMEM, SMEM, VMEM],
        out_specs=[VMEM, VMEM, VMEM],
        out_shape=[
            jax.ShapeDtypeStruct((levels, 2 * length, length), BF16),
            jax.ShapeDtypeStruct((levels, 64, length), BF16),
            jax.ShapeDtypeStruct((128, levels * length), BF16),
        ],
        scratch_shapes=[
            pltpu.VMEM((4, 128, 128), F32),
            pltpu.VMEM((128, 128), F32),
            pltpu.VMEM((length, levels, 256), F32),
            pltpu.VMEM((length, levels, 256), F32),
            pltpu.VMEM((length, 4, levels, 128), F32),
        ],
        compiler_params=pltpu.CompilerParams(vmem_limit_bytes=16 * MIB),
        cost_estimate=pl.CostEstimate(flops=2_000_000_000, bytes_accessed=4 * MIB, transcendentals=0),
        name="east_matrices",
    )(place, taps, east_filter)


def north_finish(own, edges, entered, sends):
    levels = edges.shape[0]
    pairs = entered.shape[1] // 16

    def kernel(c0_ref, b_ref, z_ref, v_ref, c_hbm, c_ref, sems):
        stores = [
            pltpu.make_async_copy(
                c_ref.at[:, pl.ds(16 * j, 16)], c_hbm.at[:, pl.ds(16 * j, 16)], sems.at[j]
            )
            for j in range(levels // 4)
        ]
        empty = jnp.zeros((16, 128), BF16)
        lefts = []
        for l in range(levels):
            values = [
                jnp.concatenate(split(z_ref[l, 16 * p : 16 * p + 16, :]), axis=1) for p in range(pairs)
            ]
            out = dot_nt(
                jnp.concatenate([v_ref[l], v_ref[l]], axis=1), jnp.concatenate(values * 2, axis=0)
            )
            high, low = split_rounded(out[0:32] + out[32:64])
            left = jnp.where(lanes_of(32) < 64, high, low).astype(BF16)
            lefts.append(jnp.concatenate([left, left], axis=1))
        for l in range(levels):
            blocks = [
                jnp.concatenate(
                    [
                        jnp.concatenate([piece if p == q else empty for q in range(pairs)], axis=1)
                        for p in range(pairs)
                    ],
                    axis=0,
                )
                for piece in (b_ref[l, 0:16], b_ref[l, 16:32])
            ]
            out = dot(lefts[l], jnp.concatenate([blocks[0], blocks[0], blocks[1], blocks[1]], axis=0))
            for e in range(8):
                at = slice(4 * l, 4 * l + 4)
                c_ref[e, at, :] = c0_ref[e, at, :] + out[4 * e : 4 * e + 4]
            if l % 4 == 3:
                stores[l // 4].start()
        for store in stores:
            store.wait()

    return pl.pallas_call(
        kernel,
        in_specs=[VMEM] * 4,
        out_specs=HBM,
        out_shape=jax.ShapeDtypeStruct(own.shape, F32),
        scratch_shapes=[pltpu.VMEM(own.shape, F32), pltpu.SemaphoreType.DMA((levels // 4,))],
        compiler_params=pltpu.CompilerParams(vmem_limit_bytes=16 * MIB),
        name="north_finish",
    )(own, edges, entered, sends)


def own_increment(taps, alpha, slab, columns, entered, east, perturbations, scale):
    members, levels, rows, width = alpha.shape

    def kernel(taps_ref, alpha_hbm, slab_ref, u_ref, z_ref, e_ref, pert_ref, out_ref, keep_ref, alpha_ref, s_ref, sem):
        fetch = pltpu.make_async_copy(alpha_hbm, alpha_ref, sem)
        fetch.start()
        fetch.wait()
        for l in range(levels):
            added = dot(u_ref[l], edge_right(z_ref, l, members))
            for first, out in north_slab(slab_left(slab_ref[:, l, :]), alpha_ref, l, members):
                out = out + added[:, width * first : width * (first + 4)]
                field = jnp.concatenate([out[:, width * m : width * m + width] for m in range(4)], axis=0)
                high, low = split(field)
                e_high = e_ref[l, 0:width]
                s_ref[l, rows * first : rows * (first + 4)] = dot(
                    jnp.concatenate([high, low], axis=1), jnp.concatenate([e_high, e_high], axis=0)
                ) + dot(high, e_ref[l, width : 2 * width])
        tap = [taps_ref[o] * scale for o in range(5)]
        for k in range(levels):
            total = jnp.zeros((rows, width), F32)
            for m in range(members):
                mixed = sum(
                    tap[o] * s_ref[k + o - 2, rows * m : rows * m + rows, :]
                    for o in range(5)
                    if 0 <= k + o - 2 < levels
                )
                total = total + pert_ref[m, k].astype(F32) * mixed
            out_ref[k] = total
        keep_ref[...] = pert_ref[...]

    return pl.pallas_call(
        kernel,
        in_specs=[SMEM, HBM] + [VMEM] * 5,
        out_specs=[VMEM, VMEM],
        out_shape=[
            jax.ShapeDtypeStruct((levels, rows, width), F32),
            jax.ShapeDtypeStruct(perturbations.shape, BF16),
        ],
        scratch_shapes=[
            pltpu.VMEM(alpha.shape, F32),
            pltpu.VMEM((levels, members * rows, width), F32),
            pltpu.SemaphoreType.DMA,
        ],
        compiler_params=pltpu.CompilerParams(vmem_limit_bytes=51 * MIB),
        cost_estimate=pl.CostEstimate(flops=2_000_000_000, bytes_accessed=4 * MIB, transcendentals=0),
        name="own_increment",
    )(taps, alpha, slab, columns, entered, east, perturbations)


def finish(place, received, columns, perturbations, partial):
    members, levels, rows, width = perturbations.shape
    slabs = received.shape[0]

    def kernel(e_ref, r_ref, w_ref, pert_ref, part_ref, out_ref):
        me = e_ref[0]
        entering = jnp.zeros(r_ref.shape[1:], F32)
        pending = jnp.zeros(r_ref.shape[1:], F32)
        for s in range(slabs):
            block = r_ref[s]
            entering = entering + jnp.where(s < me, block, 0.0)
            pending = pending + jnp.where(s > me, block, 0.0)
        edge = jnp.concatenate([entering, pending] * 2, axis=0).T
        high, low = split_rounded(edge)
        left = jnp.where(lanes_of(members * rows) < 64, high, low).astype(BF16)
        left = jnp.concatenate([left, left], axis=1)
        for k in range(levels):
            out_ref[k] = part_ref[k]
        high, low = w_ref[0:64], w_ref[64:128]
        right = jnp.concatenate([high, high, low, low], axis=0)
        for m in range(members):
            added = dot(left[rows * m : rows * m + rows], right)
            for k in range(levels):
                out_ref[k] += pert_ref[m, k].astype(F32) * added[:, width * k : width * k + width]

    return pl.pallas_call(
        kernel,
        in_specs=[SMEM] + [VMEM] * 4,
        out_specs=VMEM,
        out_shape=jax.ShapeDtypeStruct((levels, rows, width), F32),
        compiler_params=pltpu.CompilerParams(vmem_limit_bytes=16 * MIB),
        name="finish",
    )(place, received, columns, perturbations, partial)


def local(alpha_fields, perturbations, north_filter, east_filter, depth_taps):
    members, levels, rows, width = alpha_fields.shape
    scale = 1.0 / math.sqrt(members * lax.axis_size("group") - 1)
    place = jnp.full((1,), lax.axis_index("east"), jnp.int32)
    functionals, slab = north_functionals(levels, members, rows)(north_filter, alpha_fields)
    gathered = lax.all_to_all(functionals, "north", 0, 0)
    east, sends, columns = east_matrices(place, depth_taps, east_filter, scale)
    gathered, sends = lax.optimization_barrier((gathered, sends))
    chained, slab = lax.optimization_barrier((chain_slabs(gathered), slab))
    entered = lax.all_to_all(chained, "north", 0, 0).reshape(levels, 8 * members, width)
    own, edge, blocks = own_crossing(alpha_fields, slab, sends)
    crossing = north_finish(own, blocks, entered, sends)
    crossing, entered = lax.optimization_barrier((crossing, entered))
    crossed = lax.all_to_all(crossing, "east", 0, 0)
    partial, kept = own_increment(depth_taps, alpha_fields, slab, edge, entered, east, perturbations, scale)
    increment = finish(place, crossed, columns, kept, partial)
    return increment + lax.ppermute(increment, "group", [(0, 1), (1, 0)])


def solution(mesh):
    placed = (
        P("group", None, "north", "east"),
        P("group", None, "north", "east"),
        P(None, None, "north"),
        P(),
        P(),
    )
    return jax.shard_map(
        local, mesh=mesh, in_specs=placed, out_specs=P(None, "north", "east"), check_vma=False
    )
```

```python
import math

import jax
import jax.numpy as jnp
from jax import lax
from jax.experimental import pallas as pl
from jax.experimental.pallas import tpu as pltpu
from jax.sharding import PartitionSpec as P

F32 = jnp.float32
BF16 = jnp.bfloat16
VMEM = pl.BlockSpec(memory_space=pltpu.VMEM)
SMEM = pl.BlockSpec(memory_space=pltpu.SMEM)
HBM = pl.BlockSpec(memory_space=pltpu.HBM)
MIB = 1 << 20


def split(x):
    high = x.astype(BF16)
    return high, (x - high.astype(F32)).astype(BF16)


def split_rounded(x):
    high = x.astype(BF16).astype(F32)
    return high, x - high


def dot(a, b):
    return jnp.dot(a, b, preferred_element_type=F32)


def dot_nt(a, b):
    return lax.dot_general(a, b, (((1,), (1,)), ((), ())), preferred_element_type=F32)


def wide(column, lanes=128):
    return jnp.broadcast_to(column, (column.shape[0], lanes))


def lanes_of(rows=8, lanes=128):
    return lax.broadcasted_iota(jnp.int32, (rows, lanes), 1)


def rows_of(rows=8, lanes=128):
    return lax.broadcasted_iota(jnp.int32, (rows, lanes), 0)


def copies(source, target, sems, count):
    return [pltpu.make_async_copy(source.at[i], target.at[i], sems.at[i]) for i in range(count)]


def unit(mask):
    return jnp.where(mask, 1.0, 0.0).astype(F32)


def north_functionals(levels, members, rows):
    def kernel(
        nf_hbm, alpha_hbm, p_hbm, s_hbm, nf_ref, alpha_ref, f_ref, s_ref, p_ref, w_ref, nf_sem, s_sem, sem, p_sems
    ):
        table_fetch = pltpu.make_async_copy(nf_hbm, nf_ref, nf_sem)
        table_fetch.start()
        fetch = pltpu.make_async_copy(alpha_hbm, alpha_ref, sem)
        stores = copies(p_ref, p_hbm, p_sems, 2 * levels)
        slab_store = pltpu.make_async_copy(s_ref, s_hbm, s_sem)
        fetch.start()
        table_fetch.wait()
        lane = lanes_of()
        table = [nf_ref[j] for j in range(5)]
        gain = jnp.concatenate([jnp.zeros((levels, 64), F32), table[0]], axis=1)
        state = [unit(lane == k) for k in range(4)]
        for i in range(rows):
            value = jnp.where(lane == 64 + i, gain, 0.0)
            for j in (4, 3, 2, 1):
                weight = wide(table[j][:, i : i + 1])
                w_ref[i, j - 1] = weight
                value = value + weight * state[j - 1]
            f_ref[i] = value + unit(lane == 4 + rows - 1 - i) if i >= rows - 4 else value
            state = [value] + state[:3]
        state = [jnp.zeros((levels, 128), F32)] * 4
        for i in reversed(range(rows)):
            value = f_ref[i]
            for j in (4, 3, 2, 1):
                if i + j < rows:
                    value = value + w_ref[i + j, j - 1] * state[j - 1]
            s_ref[i] = value * wide(table[0][:, i : i + 1])
            state = [value] + state[:3]
        slab_store.start()
        lefts = []
        for l in range(levels):
            flat = f_ref[:, l, :]
            maps = jnp.dot(
                flat.T[0:8], flat, precision=lax.Precision.HIGHEST, preferred_element_type=F32
            )
            p_ref[2 * l, 32:40, :] = maps
            p_ref[2 * l + 1, 32:40, :] = maps
            edge = s_ref[:, l, :].T[0:8]
            high, low = split_rounded(jnp.concatenate([edge, edge], axis=1))
            lefts.append(jnp.concatenate([high, low], axis=0).astype(BF16))
        fetch.wait()
        for l in range(levels):
            for half in range(2):
                right = []
                for m in range(4):
                    a_high, a_low = split(alpha_ref[half * 4 + m, l])
                    right.append(jnp.concatenate([a_high, a_low], axis=0))
                out = dot(lefts[l], jnp.concatenate(right, axis=1))
                out = out[0:8] + out[8:16]
                for m in range(4):
                    p_ref[2 * l + half, 8 * m : 8 * m + 8, :] = out[:, 128 * m : 128 * m + 128]
                stores[2 * l + half].start()
        for store in stores + [slab_store]:
            store.wait()

    def call(north_filter, alpha):
        return pl.pallas_call(
            kernel,
            in_specs=[HBM, HBM],
            out_specs=[HBM, HBM],
            out_shape=[
                jax.ShapeDtypeStruct((2 * levels, 40, 128), F32),
                jax.ShapeDtypeStruct((rows, levels, 128), F32),
            ],
            scratch_shapes=[
                pltpu.VMEM(north_filter.shape, F32),
                pltpu.VMEM(alpha.shape, F32),
                pltpu.VMEM((rows, levels, 128), F32),
                pltpu.VMEM((rows, levels, 128), F32),
                pltpu.VMEM((2 * levels, 40, 128), F32),
                pltpu.VMEM((rows, 4, levels, 128), F32),
                pltpu.SemaphoreType.DMA,
                pltpu.SemaphoreType.DMA,
                pltpu.SemaphoreType.DMA,
                pltpu.SemaphoreType.DMA((2 * levels,)),
            ],
            compiler_params=pltpu.CompilerParams(vmem_limit_bytes=63 * MIB),
            name="north_functionals",
        )(north_filter, alpha)

    return call


def chain_slabs(received):
    slabs = received.shape[0]

    def kernel(r_ref, z_ref, v_ref):
        state = [jnp.zeros((4, 128), F32)] * 4
        for n in range(slabs):
            maps = r_ref[n, 32:40, :]
            column = [wide(maps[:, j : j + 1]) for j in range(4)]
            for m in range(4):
                z_ref[n, 8 * m : 8 * m + 4, :] = state[m]
                value = r_ref[n, 8 * m : 8 * m + 8, :]
                for j in range(4):
                    value = value + column[j] * jnp.broadcast_to(state[m][j : j + 1], (8, 128))
                v_ref[n, 4 * m : 4 * m + 4, :] = value[0:4]
                state[m] = value[4:8]
        pending = [jnp.zeros((4, 128), F32)] * 4
        for n in reversed(range(slabs)):
            maps = r_ref[n, 32:36, :]
            column = [wide(maps[:, 4 + j : 5 + j]) for j in range(4)]
            for m in range(4):
                z_ref[n, 8 * m + 4 : 8 * m + 8, :] = pending[m]
                value = v_ref[n, 4 * m : 4 * m + 4, :]
                for j in range(4):
                    value = value + column[j] * jnp.broadcast_to(pending[m][j : j + 1], (4, 128))
                pending[m] = value

    return pl.pallas_call(
        kernel,
        in_specs=[VMEM],
        out_specs=VMEM,
        out_shape=jax.ShapeDtypeStruct((slabs, 32, 128), F32),
        scratch_shapes=[pltpu.VMEM((slabs, 16, 128), F32)],
        compiler_params=pltpu.CompilerParams(vmem_limit_bytes=8 * MIB),
        name="chain_slabs",
    )(received)


def north_slab(left, alpha_ref, l, members):
    for first in range(0, members, 4):
        right = []
        for m in range(first, first + 4):
            high, low = split(alpha_ref[m, l])
            right.append(jnp.concatenate([high, low, high, low], axis=0))
        yield first, dot(left, jnp.concatenate(right, axis=1))


def slab_left(full):
    twice = jnp.where(lanes_of(full.shape[0]) < 64, pltpu.roll(full, 64, 1), full)
    high, low = split(twice)
    return jnp.concatenate([high, low], axis=1)


def edge_right(z_ref, l, members):
    right = []
    for m in range(members):
        high, low = split_rounded(z_ref[l, 8 * m : 8 * m + 8, :])
        right.append(jnp.concatenate([high, low, high, low], axis=0).astype(BF16))
    return jnp.concatenate(right, axis=1)


def crossing_rows(v_ref, l, fields):
    parts = jnp.concatenate([jnp.concatenate(split(field), axis=1) for field in fields], axis=0)
    out = dot_nt(jnp.concatenate([v_ref[l], v_ref[l]], axis=1), parts)
    return out[0:32] + out[32:64]


def own_crossing(alpha, slab, sends):
    members, levels, rows, width = alpha.shape

    def kernel(alpha_hbm, s_ref, v_ref, c_ref, u_ref, b_ref, alpha_ref, sem):
        fetch = pltpu.make_async_copy(alpha_hbm, alpha_ref, sem)
        fetch.start()
        fetch.wait()
        lane = lanes_of()
        for l in range(levels):
            full = s_ref[:, l, :]
            fields = []
            for _, out in north_slab(slab_left(full), alpha_ref, l, members):
                fields += [out[:, width * m : width * m + width] for m in range(4)]
            out = crossing_rows(v_ref, l, fields)
            for e in range(8):
                c_ref[e, 4 * l : 4 * l + 4, :] = out[4 * e : 4 * e + 4]
            high, low = split_rounded(full[:, 0:8])
            u_ref[l] = jnp.concatenate([high, high, low, low], axis=1).astype(BF16)
            edge = full.T[0:8]
            edge = jnp.concatenate([edge, edge], axis=1)
            edge = jnp.concatenate([jnp.where(lane < 64, edge, 0.0), jnp.where(lane < 64, 0.0, edge)], axis=0)
            b_ref[l] = jnp.concatenate(split(edge), axis=0)

    return pl.pallas_call(
        kernel,
        in_specs=[HBM, VMEM, VMEM],
        out_specs=[VMEM] * 3,
        scratch_shapes=[pltpu.VMEM(alpha.shape, F32), pltpu.SemaphoreType.DMA],
        out_shape=[
            jax.ShapeDtypeStruct((8, 4 * levels, members * rows), F32),
            jax.ShapeDtypeStruct((levels, rows, 32), BF16),
            jax.ShapeDtypeStruct((levels, 32, 128), BF16),
        ],
        compiler_params=pltpu.CompilerParams(vmem_limit_bytes=51 * MIB),
        cost_estimate=pl.CostEstimate(flops=2_000_000_000, bytes_accessed=4 * MIB, transcendentals=0),
        name="own_crossing",
    )(alpha, slab, sends)


def east_matrices(place, taps, east_filter, scale):
    levels = east_filter.shape[1]
    length = 128
    slabs = east_filter.shape[2] // length

    def kernel(e_ref, taps_ref, ef_ref, e_out, v_out, w_out, wt_ref, rt_ref, f_ref, s_ref, near_ref):
        me = e_ref[0]
        lane = lanes_of()
        row = rows_of()
        for j in range(1, 5):
            stacked = jnp.concatenate(
                [ef_ref[j, :, length * s : length * (s + 1)] for s in range(slabs)] * 2, axis=0
            )
            wt_ref[j - 1] = stacked.T
        state = [unit(row == k) for k in range(4)]
        gram = [jnp.zeros((8, 128), F32)] * 4
        for i in range(length):
            value = jnp.zeros((8, 128), F32)
            for j in (3, 2, 1, 0):
                value = value + jnp.broadcast_to(wt_ref[j, i : i + 1, :], (8, 128)) * state[j]
            gram = [gram[k] + value * jnp.broadcast_to(value[k : k + 1], (8, 128)) for k in range(4)]
            state = [value] + state[:3]
        step = state
        reflect = [jnp.zeros((8, 128), F32)] * 4
        for _ in range(slabs - 1):
            inner = [
                sum(jnp.broadcast_to(reflect[i][j : j + 1], (8, 128)) * step[j] for j in range(4))
                for i in range(4)
            ]
            outer = [
                gram[a]
                + sum(jnp.broadcast_to(step[i][a : a + 1], (8, 128)) * inner[i] for i in range(4))
                for a in range(4)
            ]
            reflect = [jnp.where(lane < 56, pltpu.roll(outer[a], 120, 1), 0.0) for a in range(4)]
        rt_ref[...] = jnp.concatenate(reflect * 4, axis=0).T
        back = rt_ref[pl.ds(pl.multiple_of(me * 8, 8), 8), :]
        own = [ef_ref[j, :, pl.ds(pl.multiple_of(me * length, length), length)] for j in range(5)]
        core = [jnp.zeros((levels, 128), F32)] * 4
        side = [unit(lane == k) for k in range(4)]
        for i in range(length):
            weight = [wide(own[j][:, i : i + 1]) for j in range(1, 5)]
            for j in range(4):
                near_ref[i, j] = weight[j]
            c_value = jnp.where(lane == i, own[0], 0.0)
            s_value = jnp.zeros((levels, 128), F32)
            for j in (3, 2, 1, 0):
                c_value = c_value + weight[j] * core[j]
                s_value = s_value + weight[j] * side[j]
            f_ref[i, :, 0:128] = c_value
            f_ref[i, :, 128:256] = s_value
            core = [c_value] + core[:3]
            side = [s_value] + side[:3]
        for k in range(4):
            c_value, s_value = core[k], side[k]
            for j in range(4):
                weight = wide(back[:, 8 * k + j : 8 * k + j + 1])
                c_value = c_value + weight * core[j]
                s_value = s_value + weight * side[j]
            f_ref[length - 1 - k, :, 0:128] = c_value
            f_ref[length - 1 - k, :, 128:256] = s_value + unit(lane == 4 + k)
        core = [jnp.zeros((levels, 128), F32)] * 4
        side = [jnp.zeros((levels, 128), F32)] * 4
        for i in reversed(range(length)):
            c_value = f_ref[i, :, 0:128]
            s_value = f_ref[i, :, 128:256]
            for j in (4, 3, 2, 1):
                if i + j < length:
                    weight = near_ref[i + j, j - 1]
                    c_value = c_value + weight * core[j - 1]
                    s_value = s_value + weight * side[j - 1]
            gain = wide(own[0][:, i : i + 1])
            s_ref[i, :, 0:128] = c_value * gain
            s_ref[i, :, 128:256] = s_value * gain
            core = [c_value] + core[:3]
            side = [s_value] + side[:3]
        across = [
            jnp.concatenate([step[i][j : j + 1] for i in range(4)], axis=0) for j in range(4)
        ]
        entering, pending = [], []
        for l in range(levels):
            e_out[l] = jnp.concatenate(split(s_ref[:, l, 0:128]), axis=0)
            edge = s_ref[:, l, 128:256].T[0:8]
            entering.append(edge[0:4])
            pending.append(edge[4:8])
        upward, downward = [pending], [entering]
        for e in range(1, slabs):
            for chain, column, at, beyond, first in (
                (upward, across, e - 1, e - 1 > me, pending),
                (downward, step, slabs - e, slabs - e < me, entering),
            ):
                moved = [
                    sum(
                        wide(column[j][0:4, 8 * at + l : 8 * at + l + 1])
                        * jnp.broadcast_to(chain[-1][l][j : j + 1], (4, 128))
                        for j in range(4)
                    )
                    for l in range(levels)
                ]
                chain.append([jnp.where(beyond, moved[l], first[l]) for l in range(levels)])
        downward.reverse()
        for l in range(levels):
            sends = jnp.concatenate(
                [jnp.where(e > me, upward[e][l], downward[e][l]) for e in range(slabs)], axis=0
            )
            v_out[l] = jnp.concatenate(split_rounded(sends), axis=0).astype(BF16)
        columns = jnp.concatenate(entering + pending, axis=0)
        level = lax.rem(rows_of(64), 32) // 4
        for k in range(levels):
            mix = jnp.zeros((64, 128), F32)
            for offset in range(5):
                mix = mix + jnp.where(level - k == offset - 2, taps_ref[offset] * scale, 0.0)
            high, low = split(columns * mix)
            w_out[:, 128 * k : 128 * k + 128] = jnp.concatenate([high, low], axis=0)

    return pl.pallas_call(
        kernel,
        in_specs=[SMEM, SMEM, VMEM],
        out_specs=[VMEM, VMEM, VMEM],
        out_shape=[
            jax.ShapeDtypeStruct((levels, 2 * length, length), BF16),
            jax.ShapeDtypeStruct((levels, 64, length), BF16),
            jax.ShapeDtypeStruct((128, levels * length), BF16),
        ],
        scratch_shapes=[
            pltpu.VMEM((4, 128, 128), F32),
            pltpu.VMEM((128, 128), F32),
            pltpu.VMEM((length, levels, 256), F32),
            pltpu.VMEM((length, levels, 256), F32),
            pltpu.VMEM((length, 4, levels, 128), F32),
        ],
        compiler_params=pltpu.CompilerParams(vmem_limit_bytes=16 * MIB),
        cost_estimate=pl.CostEstimate(flops=2_000_000_000, bytes_accessed=4 * MIB, transcendentals=0),
        name="east_matrices",
    )(place, taps, east_filter)


def north_finish(own, edges, entered, sends):
    levels = edges.shape[0]
    pairs = entered.shape[1] // 16

    def kernel(c0_ref, b_ref, z_ref, v_ref, c_hbm, c_ref, sems):
        stores = [
            pltpu.make_async_copy(
                c_ref.at[:, pl.ds(16 * j, 16)], c_hbm.at[:, pl.ds(16 * j, 16)], sems.at[j]
            )
            for j in range(levels // 4)
        ]
        empty = jnp.zeros((16, 128), BF16)
        lefts = []
        for l in range(levels):
            values = [
                jnp.concatenate(split(z_ref[l, 16 * p : 16 * p + 16, :]), axis=1) for p in range(pairs)
            ]
            out = dot_nt(
                jnp.concatenate([v_ref[l], v_ref[l]], axis=1), jnp.concatenate(values * 2, axis=0)
            )
            high, low = split_rounded(out[0:32] + out[32:64])
            left = jnp.where(lanes_of(32) < 64, high, low).astype(BF16)
            lefts.append(jnp.concatenate([left, left], axis=1))
        for l in range(levels):
            blocks = [
                jnp.concatenate(
                    [
                        jnp.concatenate([piece if p == q else empty for q in range(pairs)], axis=1)
                        for p in range(pairs)
                    ],
                    axis=0,
                )
                for piece in (b_ref[l, 0:16], b_ref[l, 16:32])
            ]
            out = dot(lefts[l], jnp.concatenate([blocks[0], blocks[0], blocks[1], blocks[1]], axis=0))
            for e in range(8):
                at = slice(4 * l, 4 * l + 4)
                c_ref[e, at, :] = c0_ref[e, at, :] + out[4 * e : 4 * e + 4]
            if l % 4 == 3:
                stores[l // 4].start()
        for store in stores:
            store.wait()

    return pl.pallas_call(
        kernel,
        in_specs=[VMEM] * 4,
        out_specs=HBM,
        out_shape=jax.ShapeDtypeStruct(own.shape, F32),
        scratch_shapes=[pltpu.VMEM(own.shape, F32), pltpu.SemaphoreType.DMA((levels // 4,))],
        compiler_params=pltpu.CompilerParams(vmem_limit_bytes=16 * MIB),
        name="north_finish",
    )(own, edges, entered, sends)


def own_increment(taps, alpha, slab, columns, entered, east, perturbations, scale):
    members, levels, rows, width = alpha.shape

    def kernel(taps_ref, alpha_hbm, slab_ref, u_ref, z_ref, e_ref, pert_ref, out_ref, keep_ref, alpha_ref, s_ref, sem):
        fetch = pltpu.make_async_copy(alpha_hbm, alpha_ref, sem)
        fetch.start()
        fetch.wait()
        for l in range(levels):
            added = dot(u_ref[l], edge_right(z_ref, l, members))
            for first, out in north_slab(slab_left(slab_ref[:, l, :]), alpha_ref, l, members):
                out = out + added[:, width * first : width * (first + 4)]
                field = jnp.concatenate([out[:, width * m : width * m + width] for m in range(4)], axis=0)
                high, low = split(field)
                e_high = e_ref[l, 0:width]
                s_ref[l, rows * first : rows * (first + 4)] = dot(
                    jnp.concatenate([high, low], axis=1), jnp.concatenate([e_high, e_high], axis=0)
                ) + dot(high, e_ref[l, width : 2 * width])
        tap = [taps_ref[o] * scale for o in range(5)]
        for k in range(levels):
            total = jnp.zeros((rows, width), F32)
            for m in range(members):
                mixed = sum(
                    tap[o] * s_ref[k + o - 2, rows * m : rows * m + rows, :]
                    for o in range(5)
                    if 0 <= k + o - 2 < levels
                )
                total = total + pert_ref[m, k].astype(F32) * mixed
            out_ref[k] = total
        keep_ref[...] = pert_ref[...]

    return pl.pallas_call(
        kernel,
        in_specs=[SMEM, HBM] + [VMEM] * 5,
        out_specs=[VMEM, VMEM],
        out_shape=[
            jax.ShapeDtypeStruct((levels, rows, width), F32),
            jax.ShapeDtypeStruct(perturbations.shape, BF16),
        ],
        scratch_shapes=[
            pltpu.VMEM(alpha.shape, F32),
            pltpu.VMEM((levels, members * rows, width), F32),
            pltpu.SemaphoreType.DMA,
        ],
        compiler_params=pltpu.CompilerParams(vmem_limit_bytes=51 * MIB),
        cost_estimate=pl.CostEstimate(flops=2_000_000_000, bytes_accessed=4 * MIB, transcendentals=0),
        name="own_increment",
    )(taps, alpha, slab, columns, entered, east, perturbations)


def finish(place, received, columns, perturbations, partial):
    members, levels, rows, width = perturbations.shape
    slabs = received.shape[0]

    def kernel(e_ref, r_ref, w_ref, pert_ref, part_ref, out_ref):
        me = e_ref[0]
        entering = jnp.zeros(r_ref.shape[1:], F32)
        pending = jnp.zeros(r_ref.shape[1:], F32)
        for s in range(slabs):
            block = r_ref[s]
            entering = entering + jnp.where(s < me, block, 0.0)
            pending = pending + jnp.where(s > me, block, 0.0)
        edge = jnp.concatenate([entering, pending] * 2, axis=0).T
        high, low = split_rounded(edge)
        left = jnp.where(lanes_of(members * rows) < 64, high, low).astype(BF16)
        left = jnp.concatenate([left, left], axis=1)
        high, low = w_ref[0:64], w_ref[64:128]
        right = jnp.concatenate([high, high, low, low], axis=0)
        for first in range(0, levels, 2):
            added = dot(left, right[:, width * first : width * (first + 2)])
            for k in range(first, first + 2):
                total = part_ref[k]
                for m in range(members):
                    block = added[rows * m : rows * m + rows, width * (k - first) : width * (k - first + 1)]
                    total = total + pert_ref[m, k].astype(F32) * block
                out_ref[k] = total

    return pl.pallas_call(
        kernel,
        in_specs=[SMEM] + [VMEM] * 4,
        out_specs=VMEM,
        out_shape=jax.ShapeDtypeStruct((levels, rows, width), F32),
        compiler_params=pltpu.CompilerParams(vmem_limit_bytes=16 * MIB),
        name="finish",
    )(place, received, columns, perturbations, partial)


def local(alpha_fields, perturbations, north_filter, east_filter, depth_taps):
    members, levels, rows, width = alpha_fields.shape
    scale = 1.0 / math.sqrt(members * lax.axis_size("group") - 1)
    place = jnp.full((1,), lax.axis_index("east"), jnp.int32)
    functionals, slab = north_functionals(levels, members, rows)(north_filter, alpha_fields)
    gathered = lax.all_to_all(functionals, "north", 0, 0)
    east, sends, columns = east_matrices(place, depth_taps, east_filter, scale)
    gathered, sends = lax.optimization_barrier((gathered, sends))
    chained, slab = lax.optimization_barrier((chain_slabs(gathered), slab))
    entered = lax.all_to_all(chained, "north", 0, 0).reshape(levels, 8 * members, width)
    own, edge, blocks = own_crossing(alpha_fields, slab, sends)
    crossing = north_finish(own, blocks, entered, sends)
    crossing, entered = lax.optimization_barrier((crossing, entered))
    crossed = lax.all_to_all(crossing, "east", 0, 0)
    partial, kept = own_increment(depth_taps, alpha_fields, slab, edge, entered, east, perturbations, scale)
    increment = finish(place, crossed, columns, kept, partial)
    return increment + lax.ppermute(increment, "group", [(0, 1), (1, 0)])


def solution(mesh):
    placed = (
        P("group", None, "north", "east"),
        P("group", None, "north", "east"),
        P(None, None, "north"),
        P(),
        P(),
    )
    return jax.shard_map(
        local, mesh=mesh, in_specs=placed, out_specs=P(None, "north", "east"), check_vma=False
    )
```

```python
import math

import jax
import jax.numpy as jnp
from jax import lax
from jax.experimental import pallas as pl
from jax.experimental.pallas import tpu as pltpu
from jax.sharding import PartitionSpec as P

F32 = jnp.float32
BF16 = jnp.bfloat16
VMEM = pl.BlockSpec(memory_space=pltpu.VMEM)
SMEM = pl.BlockSpec(memory_space=pltpu.SMEM)
HBM = pl.BlockSpec(memory_space=pltpu.HBM)
MIB = 1 << 20


def split(x):
    high = x.astype(BF16)
    return high, (x - high.astype(F32)).astype(BF16)


def split_rounded(x):
    high = x.astype(BF16).astype(F32)
    return high, x - high


def dot(a, b):
    return jnp.dot(a, b, preferred_element_type=F32)


def dot_nt(a, b):
    return lax.dot_general(a, b, (((1,), (1,)), ((), ())), preferred_element_type=F32)


def wide(column, lanes=128):
    return jnp.broadcast_to(column, (column.shape[0], lanes))


def lanes_of(rows=8, lanes=128):
    return lax.broadcasted_iota(jnp.int32, (rows, lanes), 1)


def rows_of(rows=8, lanes=128):
    return lax.broadcasted_iota(jnp.int32, (rows, lanes), 0)


def copies(source, target, sems, count):
    return [pltpu.make_async_copy(source.at[i], target.at[i], sems.at[i]) for i in range(count)]


def unit(mask):
    return jnp.where(mask, 1.0, 0.0).astype(F32)


def north_functionals(levels, members, rows):
    def kernel(
        nf_hbm, alpha_hbm, p_hbm, s_hbm, nf_ref, alpha_ref, f_ref, s_ref, p_ref, w_ref, nf_sem, s_sem, sem, p_sems
    ):
        table_fetch = pltpu.make_async_copy(nf_hbm, nf_ref, nf_sem)
        table_fetch.start()
        fetch = pltpu.make_async_copy(alpha_hbm, alpha_ref, sem)
        stores = copies(p_ref, p_hbm, p_sems, 2 * levels)
        slab_store = pltpu.make_async_copy(s_ref, s_hbm, s_sem)
        fetch.start()
        table_fetch.wait()
        lane = lanes_of()
        table = [nf_ref[j] for j in range(5)]
        gain = jnp.concatenate([jnp.zeros((levels, 64), F32), table[0]], axis=1)
        state = [unit(lane == k) for k in range(4)]
        for i in range(rows):
            value = jnp.where(lane == 64 + i, gain, 0.0)
            for j in (4, 3, 2, 1):
                weight = wide(table[j][:, i : i + 1])
                w_ref[i, j - 1] = weight
                value = value + weight * state[j - 1]
            f_ref[i] = value + unit(lane == 4 + rows - 1 - i) if i >= rows - 4 else value
            state = [value] + state[:3]
        state = [jnp.zeros((levels, 128), F32)] * 4
        for i in reversed(range(rows)):
            value = f_ref[i]
            for j in (4, 3, 2, 1):
                if i + j < rows:
                    value = value + w_ref[i + j, j - 1] * state[j - 1]
            s_ref[i] = value * wide(table[0][:, i : i + 1])
            state = [value] + state[:3]
        slab_store.start()
        lefts = []
        for l in range(levels):
            flat = f_ref[:, l, :]
            maps = jnp.dot(
                flat.T[0:8], flat, precision=lax.Precision.HIGHEST, preferred_element_type=F32
            )
            p_ref[2 * l, 32:40, :] = maps
            p_ref[2 * l + 1, 32:40, :] = maps
            edge = s_ref[:, l, :].T[0:8]
            high, low = split_rounded(jnp.concatenate([edge, edge], axis=1))
            lefts.append(jnp.concatenate([high, low], axis=0).astype(BF16))
        fetch.wait()
        for l in range(levels):
            for half in range(2):
                right = []
                for m in range(4):
                    a_high, a_low = split(alpha_ref[half * 4 + m, l])
                    right.append(jnp.concatenate([a_high, a_low], axis=0))
                out = dot(lefts[l], jnp.concatenate(right, axis=1))
                out = out[0:8] + out[8:16]
                for m in range(4):
                    p_ref[2 * l + half, 8 * m : 8 * m + 8, :] = out[:, 128 * m : 128 * m + 128]
                stores[2 * l + half].start()
        for store in stores + [slab_store]:
            store.wait()

    def call(north_filter, alpha):
        return pl.pallas_call(
            kernel,
            in_specs=[HBM, HBM],
            out_specs=[HBM, HBM],
            out_shape=[
                jax.ShapeDtypeStruct((2 * levels, 40, 128), F32),
                jax.ShapeDtypeStruct((rows, levels, 128), F32),
            ],
            scratch_shapes=[
                pltpu.VMEM(north_filter.shape, F32),
                pltpu.VMEM(alpha.shape, F32),
                pltpu.VMEM((rows, levels, 128), F32),
                pltpu.VMEM((rows, levels, 128), F32),
                pltpu.VMEM((2 * levels, 40, 128), F32),
                pltpu.VMEM((rows, 4, levels, 128), F32),
                pltpu.SemaphoreType.DMA,
                pltpu.SemaphoreType.DMA,
                pltpu.SemaphoreType.DMA,
                pltpu.SemaphoreType.DMA((2 * levels,)),
            ],
            compiler_params=pltpu.CompilerParams(vmem_limit_bytes=63 * MIB),
            name="north_functionals",
        )(north_filter, alpha)

    return call


def chain_slabs(received):
    slabs = received.shape[0]

    group = slabs // 4

    def kernel(r_ref, z_hbm, z_ref, v_ref, sems):
        stores = [
            pltpu.make_async_copy(
                z_ref.at[pl.ds(group * j, group)], z_hbm.at[pl.ds(group * j, group)], sems.at[j]
            )
            for j in range(4)
        ]
        state = [jnp.zeros((4, 128), F32)] * 4
        for n in range(slabs):
            maps = r_ref[n, 32:40, :]
            column = [wide(maps[:, j : j + 1]) for j in range(4)]
            for m in range(4):
                z_ref[n, 8 * m : 8 * m + 4, :] = state[m]
                value = r_ref[n, 8 * m : 8 * m + 8, :]
                for j in range(4):
                    value = value + column[j] * jnp.broadcast_to(state[m][j : j + 1], (8, 128))
                v_ref[n, 4 * m : 4 * m + 4, :] = value[0:4]
                state[m] = value[4:8]
        pending = [jnp.zeros((4, 128), F32)] * 4
        for n in reversed(range(slabs)):
            maps = r_ref[n, 32:36, :]
            column = [wide(maps[:, 4 + j : 5 + j]) for j in range(4)]
            for m in range(4):
                z_ref[n, 8 * m + 4 : 8 * m + 8, :] = pending[m]
                value = v_ref[n, 4 * m : 4 * m + 4, :]
                for j in range(4):
                    value = value + column[j] * jnp.broadcast_to(pending[m][j : j + 1], (4, 128))
                pending[m] = value
            if n % group == 0:
                stores[n // group].start()
        for store in stores:
            store.wait()

    return pl.pallas_call(
        kernel,
        in_specs=[VMEM],
        out_specs=HBM,
        out_shape=jax.ShapeDtypeStruct((slabs, 32, 128), F32),
        scratch_shapes=[
            pltpu.VMEM((slabs, 32, 128), F32),
            pltpu.VMEM((slabs, 16, 128), F32),
            pltpu.SemaphoreType.DMA((4,)),
        ],
        compiler_params=pltpu.CompilerParams(vmem_limit_bytes=8 * MIB),
        name="chain_slabs",
    )(received)


def north_slab(left, alpha_ref, l, members):
    for first in range(0, members, 4):
        right = []
        for m in range(first, first + 4):
            high, low = split(alpha_ref[m, l])
            right.append(jnp.concatenate([high, low, high, low], axis=0))
        yield first, dot(left, jnp.concatenate(right, axis=1))


def slab_left(full):
    twice = jnp.where(lanes_of(full.shape[0]) < 64, pltpu.roll(full, 64, 1), full)
    high, low = split(twice)
    return jnp.concatenate([high, low], axis=1)


def edge_right(z_ref, l, members):
    right = []
    for m in range(members):
        high, low = split_rounded(z_ref[l, 8 * m : 8 * m + 8, :])
        right.append(jnp.concatenate([high, low, high, low], axis=0).astype(BF16))
    return jnp.concatenate(right, axis=1)


def crossing_rows(v_ref, l, fields):
    parts = jnp.concatenate([jnp.concatenate(split(field), axis=1) for field in fields], axis=0)
    out = dot_nt(jnp.concatenate([v_ref[l], v_ref[l]], axis=1), parts)
    return out[0:32] + out[32:64]


def own_crossing(alpha, slab, sends):
    members, levels, rows, width = alpha.shape

    def kernel(alpha_hbm, s_ref, v_ref, c_ref, u_ref, b_ref, alpha_ref, sem):
        fetch = pltpu.make_async_copy(alpha_hbm, alpha_ref, sem)
        fetch.start()
        fetch.wait()
        lane = lanes_of()
        for l in range(levels):
            full = s_ref[:, l, :]
            fields = []
            for _, out in north_slab(slab_left(full), alpha_ref, l, members):
                fields += [out[:, width * m : width * m + width] for m in range(4)]
            out = crossing_rows(v_ref, l, fields)
            for e in range(8):
                c_ref[e, 4 * l : 4 * l + 4, :] = out[4 * e : 4 * e + 4]
            high, low = split_rounded(full[:, 0:8])
            u_ref[l] = jnp.concatenate([high, high, low, low], axis=1).astype(BF16)
            edge = full.T[0:8]
            edge = jnp.concatenate([edge, edge], axis=1)
            edge = jnp.concatenate([jnp.where(lane < 64, edge, 0.0), jnp.where(lane < 64, 0.0, edge)], axis=0)
            b_ref[l] = jnp.concatenate(split(edge), axis=0)

    return pl.pallas_call(
        kernel,
        in_specs=[HBM, VMEM, VMEM],
        out_specs=[VMEM] * 3,
        scratch_shapes=[pltpu.VMEM(alpha.shape, F32), pltpu.SemaphoreType.DMA],
        out_shape=[
            jax.ShapeDtypeStruct((8, 4 * levels, members * rows), F32),
            jax.ShapeDtypeStruct((levels, rows, 32), BF16),
            jax.ShapeDtypeStruct((levels, 32, 128), BF16),
        ],
        compiler_params=pltpu.CompilerParams(vmem_limit_bytes=51 * MIB),
        cost_estimate=pl.CostEstimate(flops=2_000_000_000, bytes_accessed=4 * MIB, transcendentals=0),
        name="own_crossing",
    )(alpha, slab, sends)


def east_matrices(place, taps, east_filter, scale):
    levels = east_filter.shape[1]
    length = 128
    slabs = east_filter.shape[2] // length

    def kernel(e_ref, taps_ref, ef_ref, e_out, v_out, w_out, wt_ref, rt_ref, f_ref, s_ref, near_ref):
        me = e_ref[0]
        lane = lanes_of()
        row = rows_of()
        for j in range(1, 5):
            stacked = jnp.concatenate(
                [ef_ref[j, :, length * s : length * (s + 1)] for s in range(slabs)] * 2, axis=0
            )
            wt_ref[j - 1] = stacked.T
        state = [unit(row == k) for k in range(4)]
        gram = [jnp.zeros((8, 128), F32)] * 4
        for i in range(length):
            value = jnp.zeros((8, 128), F32)
            for j in (3, 2, 1, 0):
                value = value + jnp.broadcast_to(wt_ref[j, i : i + 1, :], (8, 128)) * state[j]
            gram = [gram[k] + value * jnp.broadcast_to(value[k : k + 1], (8, 128)) for k in range(4)]
            state = [value] + state[:3]
        step = state
        reflect = [jnp.zeros((8, 128), F32)] * 4
        for _ in range(slabs - 1):
            inner = [
                sum(jnp.broadcast_to(reflect[i][j : j + 1], (8, 128)) * step[j] for j in range(4))
                for i in range(4)
            ]
            outer = [
                gram[a]
                + sum(jnp.broadcast_to(step[i][a : a + 1], (8, 128)) * inner[i] for i in range(4))
                for a in range(4)
            ]
            reflect = [jnp.where(lane < 56, pltpu.roll(outer[a], 120, 1), 0.0) for a in range(4)]
        rt_ref[...] = jnp.concatenate(reflect * 4, axis=0).T
        back = rt_ref[pl.ds(pl.multiple_of(me * 8, 8), 8), :]
        own = [ef_ref[j, :, pl.ds(pl.multiple_of(me * length, length), length)] for j in range(5)]
        core = [jnp.zeros((levels, 128), F32)] * 4
        side = [unit(lane == k) for k in range(4)]
        for i in range(length):
            weight = [wide(own[j][:, i : i + 1]) for j in range(1, 5)]
            for j in range(4):
                near_ref[i, j] = weight[j]
            c_value = jnp.where(lane == i, own[0], 0.0)
            s_value = jnp.zeros((levels, 128), F32)
            for j in (3, 2, 1, 0):
                c_value = c_value + weight[j] * core[j]
                s_value = s_value + weight[j] * side[j]
            f_ref[i, :, 0:128] = c_value
            f_ref[i, :, 128:256] = s_value
            core = [c_value] + core[:3]
            side = [s_value] + side[:3]
        for k in range(4):
            c_value, s_value = core[k], side[k]
            for j in range(4):
                weight = wide(back[:, 8 * k + j : 8 * k + j + 1])
                c_value = c_value + weight * core[j]
                s_value = s_value + weight * side[j]
            f_ref[length - 1 - k, :, 0:128] = c_value
            f_ref[length - 1 - k, :, 128:256] = s_value + unit(lane == 4 + k)
        core = [jnp.zeros((levels, 128), F32)] * 4
        side = [jnp.zeros((levels, 128), F32)] * 4
        for i in reversed(range(length)):
            c_value = f_ref[i, :, 0:128]
            s_value = f_ref[i, :, 128:256]
            for j in (4, 3, 2, 1):
                if i + j < length:
                    weight = near_ref[i + j, j - 1]
                    c_value = c_value + weight * core[j - 1]
                    s_value = s_value + weight * side[j - 1]
            gain = wide(own[0][:, i : i + 1])
            s_ref[i, :, 0:128] = c_value * gain
            s_ref[i, :, 128:256] = s_value * gain
            core = [c_value] + core[:3]
            side = [s_value] + side[:3]
        across = [
            jnp.concatenate([step[i][j : j + 1] for i in range(4)], axis=0) for j in range(4)
        ]
        entering, pending = [], []
        for l in range(levels):
            e_out[l] = jnp.concatenate(split(s_ref[:, l, 0:128]), axis=0)
            edge = s_ref[:, l, 128:256].T[0:8]
            entering.append(edge[0:4])
            pending.append(edge[4:8])
        upward, downward = [pending], [entering]
        for e in range(1, slabs):
            for chain, column, at, beyond, first in (
                (upward, across, e - 1, e - 1 > me, pending),
                (downward, step, slabs - e, slabs - e < me, entering),
            ):
                moved = [
                    sum(
                        wide(column[j][0:4, 8 * at + l : 8 * at + l + 1])
                        * jnp.broadcast_to(chain[-1][l][j : j + 1], (4, 128))
                        for j in range(4)
                    )
                    for l in range(levels)
                ]
                chain.append([jnp.where(beyond, moved[l], first[l]) for l in range(levels)])
        downward.reverse()
        for l in range(levels):
            sends = jnp.concatenate(
                [jnp.where(e > me, upward[e][l], downward[e][l]) for e in range(slabs)], axis=0
            )
            v_out[l] = jnp.concatenate(split_rounded(sends), axis=0).astype(BF16)
        columns = jnp.concatenate(entering + pending, axis=0)
        level = lax.rem(rows_of(64), 32) // 4
        for k in range(levels):
            mix = jnp.zeros((64, 128), F32)
            for offset in range(5):
                mix = mix + jnp.where(level - k == offset - 2, taps_ref[offset] * scale, 0.0)
            high, low = split(columns * mix)
            w_out[:, 128 * k : 128 * k + 128] = jnp.concatenate([high, low], axis=0)

    return pl.pallas_call(
        kernel,
        in_specs=[SMEM, SMEM, VMEM],
        out_specs=[VMEM, VMEM, VMEM],
        out_shape=[
            jax.ShapeDtypeStruct((levels, 2 * length, length), BF16),
            jax.ShapeDtypeStruct((levels, 64, length), BF16),
            jax.ShapeDtypeStruct((128, levels * length), BF16),
        ],
        scratch_shapes=[
            pltpu.VMEM((4, 128, 128), F32),
            pltpu.VMEM((128, 128), F32),
            pltpu.VMEM((length, levels, 256), F32),
            pltpu.VMEM((length, levels, 256), F32),
            pltpu.VMEM((length, 4, levels, 128), F32),
        ],
        compiler_params=pltpu.CompilerParams(vmem_limit_bytes=16 * MIB),
        cost_estimate=pl.CostEstimate(flops=2_000_000_000, bytes_accessed=4 * MIB, transcendentals=0),
        name="east_matrices",
    )(place, taps, east_filter)


def north_finish(own, edges, entered, sends):
    levels = edges.shape[0]
    pairs = entered.shape[1] // 16

    def kernel(c0_ref, b_ref, z_ref, v_ref, c_hbm, c_ref, sems):
        stores = [
            pltpu.make_async_copy(
                c_ref.at[:, pl.ds(16 * j, 16)], c_hbm.at[:, pl.ds(16 * j, 16)], sems.at[j]
            )
            for j in range(levels // 4)
        ]
        empty = jnp.zeros((16, 128), BF16)
        lefts = []
        for l in range(levels):
            values = [
                jnp.concatenate(split(z_ref[l, 16 * p : 16 * p + 16, :]), axis=1) for p in range(pairs)
            ]
            out = dot_nt(
                jnp.concatenate([v_ref[l], v_ref[l]], axis=1), jnp.concatenate(values * 2, axis=0)
            )
            high, low = split_rounded(out[0:32] + out[32:64])
            left = jnp.where(lanes_of(32) < 64, high, low).astype(BF16)
            lefts.append(jnp.concatenate([left, left], axis=1))
        for l in range(levels):
            blocks = [
                jnp.concatenate(
                    [
                        jnp.concatenate([piece if p == q else empty for q in range(pairs)], axis=1)
                        for p in range(pairs)
                    ],
                    axis=0,
                )
                for piece in (b_ref[l, 0:16], b_ref[l, 16:32])
            ]
            out = dot(lefts[l], jnp.concatenate([blocks[0], blocks[0], blocks[1], blocks[1]], axis=0))
            for e in range(8):
                at = slice(4 * l, 4 * l + 4)
                c_ref[e, at, :] = c0_ref[e, at, :] + out[4 * e : 4 * e + 4]
            if l % 4 == 3:
                stores[l // 4].start()
        for store in stores:
            store.wait()

    return pl.pallas_call(
        kernel,
        in_specs=[VMEM] * 4,
        out_specs=HBM,
        out_shape=jax.ShapeDtypeStruct(own.shape, F32),
        scratch_shapes=[pltpu.VMEM(own.shape, F32), pltpu.SemaphoreType.DMA((levels // 4,))],
        compiler_params=pltpu.CompilerParams(vmem_limit_bytes=16 * MIB),
        name="north_finish",
    )(own, edges, entered, sends)


def own_increment(taps, alpha, slab, columns, entered, east, perturbations, scale):
    members, levels, rows, width = alpha.shape

    def kernel(taps_ref, alpha_hbm, slab_ref, u_ref, z_ref, e_ref, pert_ref, out_ref, keep_ref, alpha_ref, s_ref, sem):
        fetch = pltpu.make_async_copy(alpha_hbm, alpha_ref, sem)
        fetch.start()
        fetch.wait()
        for l in range(levels):
            added = dot(u_ref[l], edge_right(z_ref, l, members))
            for first, out in north_slab(slab_left(slab_ref[:, l, :]), alpha_ref, l, members):
                out = out + added[:, width * first : width * (first + 4)]
                field = jnp.concatenate([out[:, width * m : width * m + width] for m in range(4)], axis=0)
                high, low = split(field)
                e_high = e_ref[l, 0:width]
                s_ref[l, rows * first : rows * (first + 4)] = dot(
                    jnp.concatenate([high, low], axis=1), jnp.concatenate([e_high, e_high], axis=0)
                ) + dot(high, e_ref[l, width : 2 * width])
        tap = [taps_ref[o] * scale for o in range(5)]
        for k in range(levels):
            total = jnp.zeros((rows, width), F32)
            for m in range(members):
                mixed = sum(
                    tap[o] * s_ref[k + o - 2, rows * m : rows * m + rows, :]
                    for o in range(5)
                    if 0 <= k + o - 2 < levels
                )
                total = total + pert_ref[m, k].astype(F32) * mixed
            out_ref[k] = total
        keep_ref[...] = pert_ref[...]

    return pl.pallas_call(
        kernel,
        in_specs=[SMEM, HBM] + [VMEM] * 5,
        out_specs=[VMEM, VMEM],
        out_shape=[
            jax.ShapeDtypeStruct((levels, rows, width), F32),
            jax.ShapeDtypeStruct(perturbations.shape, BF16),
        ],
        scratch_shapes=[
            pltpu.VMEM(alpha.shape, F32),
            pltpu.VMEM((levels, members * rows, width), F32),
            pltpu.SemaphoreType.DMA,
        ],
        compiler_params=pltpu.CompilerParams(vmem_limit_bytes=51 * MIB),
        cost_estimate=pl.CostEstimate(flops=2_000_000_000, bytes_accessed=4 * MIB, transcendentals=0),
        name="own_increment",
    )(taps, alpha, slab, columns, entered, east, perturbations)


def finish(place, received, columns, perturbations, partial):
    members, levels, rows, width = perturbations.shape
    slabs = received.shape[0]

    def kernel(e_ref, r_ref, w_ref, pert_ref, part_ref, out_ref):
        me = e_ref[0]
        entering = jnp.zeros(r_ref.shape[1:], F32)
        pending = jnp.zeros(r_ref.shape[1:], F32)
        for s in range(slabs):
            block = r_ref[s]
            entering = entering + jnp.where(s < me, block, 0.0)
            pending = pending + jnp.where(s > me, block, 0.0)
        edge = jnp.concatenate([entering, pending] * 2, axis=0).T
        high, low = split_rounded(edge)
        left = jnp.where(lanes_of(members * rows) < 64, high, low).astype(BF16)
        left = jnp.concatenate([left, left], axis=1)
        high, low = w_ref[0:64], w_ref[64:128]
        right = jnp.concatenate([high, high, low, low], axis=0)
        for first in range(0, levels, 2):
            added = dot(left, right[:, width * first : width * (first + 2)])
            for k in range(first, first + 2):
                total = part_ref[k]
                for m in range(members):
                    block = added[rows * m : rows * m + rows, width * (k - first) : width * (k - first + 1)]
                    total = total + pert_ref[m, k].astype(F32) * block
                out_ref[k] = total

    return pl.pallas_call(
        kernel,
        in_specs=[SMEM] + [VMEM] * 4,
        out_specs=VMEM,
        out_shape=jax.ShapeDtypeStruct((levels, rows, width), F32),
        compiler_params=pltpu.CompilerParams(vmem_limit_bytes=16 * MIB),
        name="finish",
    )(place, received, columns, perturbations, partial)


def local(alpha_fields, perturbations, north_filter, east_filter, depth_taps):
    members, levels, rows, width = alpha_fields.shape
    scale = 1.0 / math.sqrt(members * lax.axis_size("group") - 1)
    place = jnp.full((1,), lax.axis_index("east"), jnp.int32)
    functionals, slab = north_functionals(levels, members, rows)(north_filter, alpha_fields)
    gathered = lax.all_to_all(functionals, "north", 0, 0)
    east, sends, columns = east_matrices(place, depth_taps, east_filter, scale)
    gathered, sends = lax.optimization_barrier((gathered, sends))
    chained, slab = lax.optimization_barrier((chain_slabs(gathered), slab))
    entered = lax.all_to_all(chained, "north", 0, 0).reshape(levels, 8 * members, width)
    own, edge, blocks = own_crossing(alpha_fields, slab, sends)
    crossing = north_finish(own, blocks, entered, sends)
    crossing, entered = lax.optimization_barrier((crossing, entered))
    crossed = lax.all_to_all(crossing, "east", 0, 0)
    partial, kept = own_increment(depth_taps, alpha_fields, slab, edge, entered, east, perturbations, scale)
    increment = finish(place, crossed, columns, kept, partial)
    return increment + lax.ppermute(increment, "group", [(0, 1), (1, 0)])


def solution(mesh):
    placed = (
        P("group", None, "north", "east"),
        P("group", None, "north", "east"),
        P(None, None, "north"),
        P(),
        P(),
    )
    return jax.shard_map(
        local, mesh=mesh, in_specs=placed, out_specs=P(None, "north", "east"), check_vma=False
    )
```
